128 devices in a mesh: src: 32 (over y, z, core), tgt: 4 (over x).
Axes of the slice: x: 4, y: 4, z: 4, core: 2. Of those that a mesh axis runs over, the one named last changes fastest.
Arguments:
- sources: bfloat16 [524288, 64], P('src'), may hold values from -2.5 to 2.5
- targets: bfloat16 [32768, 64], P('tgt'), may hold values from -2.5 to 2.5
- log_src: float32 [524288], P('src'), may hold values from -3 to 0
- log_tgt: float32 [32768], P('tgt'), may hold values from -3 to 0
- tgt_potential: float32 [32768], P('tgt'), may hold values from -6 to 6
- pattern: int32 [2048, 16], P('src'), may hold values from 0 to 127, as said below
Outputs:
- row_potential: float32 [524288], P('src')
- col_potential: float32 [32768], P('tgt')
The draws below stay inside these ranges and needn't reach their ends.
Inputs may be any that keep to these rules, and one draw needn't show every extreme that they name: `pattern`: each row holds 16 distinct block ids, and every block id is named by some row.
All inputs are finite; a program needn't handle non-finite values.
Results may differ from the reference program's by a relative error of at most 0.0003.
Values may be sent and summed in bfloat16 or wider, within the bound.
No kernel may reach another device: no remote copies, remote signals or barrier semaphores. Data moves between devices by JAX's collectives and lax.ppermute only.
A program may use at most 128 MiB of HBM per device.

```python
import jax
import jax.numpy as jnp
from jax import lax

EMB = 64
BLOCK = 256
SLOTS = 16
TB_DEV = 32
NBANDS = 2048
RECEIVER_GROUPS = 128
NS = 524288
NT = 32768


def pattern_ids(key):
    inner = jax.random.fold_in(key, 301)
    key_a, key_b, seed_element_three, key_d = jax.random.split(inner, 4)
    starting_shift = jax.random.randint(key_a, (NBANDS, RECEIVER_GROUPS), 0, 2 ** 19)
    preferred_segment = jax.random.randint(key_b, (RECEIVER_GROUPS,), 0, 4) == 0
    extra_factor = jnp.where(preferred_segment, jax.random.randint(seed_element_three, (RECEIVER_GROUPS,), 0, 2 ** 19), 0)
    order = jax.random.permutation(key_d, RECEIVER_GROUPS)
    forced = order[jnp.arange(NBANDS) % RECEIVER_GROUPS]
    receiver_indices = jnp.arange(RECEIVER_GROUPS, dtype=jnp.int32)
    segment_ratings = (starting_shift + extra_factor[None, :]) * RECEIVER_GROUPS + receiver_indices[None, :]
    segment_ratings = jnp.where(forced[:, None] == receiver_indices[None, :], 2 ** 30, segment_ratings)
    _, chosen = lax.top_k(segment_ratings.astype(jnp.int32), SLOTS)
    return chosen.astype(jnp.int32)


def target_cells(key, spread):
    inner = jax.random.fold_in(key, 201)
    key_a, key_b = jax.random.split(inner, 2)
    group_count = RECEIVER_GROUPS // TB_DEV
    ranks = jax.random.permutation(key_a, group_count)
    levels = jnp.exp(spread * (2.0 * ranks.astype(jnp.float32) / max(group_count - 1, 1) - 1.0))
    normal_part = jax.random.normal(key_b, (NT, EMB), jnp.float32)
    mixed = normal_part
    cell_level = levels[jnp.arange(NT) // (TB_DEV * BLOCK)]
    cells = jnp.clip(0.3 * mixed * cell_level[:, None], -2.5, 2.5).astype(jnp.bfloat16)
    return (cells, ranks)


def draw_pattern(key, part):
    return pattern_ids(key)


def draw_targets(key, part):
    cells, ranks = target_cells(key, 0.2)
    return cells


def draw_sources(key, part):
    chosen = pattern_ids(key)
    cells, ranks = target_cells(key, 0.2)
    key = jax.random.fold_in(key, 17)
    key_a = jax.random.fold_in(key, 0)
    seed_element_three = jax.random.fold_in(key, 2)
    key_d = jax.random.fold_in(key, 3)
    key_e = jax.random.fold_in(key, 4)
    key_f = jax.random.fold_in(key, 5)
    normal_part = jax.random.normal(key_a, (NS, EMB), jnp.float32)
    drawn = 0.3 * normal_part
    group_count = RECEIVER_GROUPS // TB_DEV
    place = jnp.arange(NS)
    chance = jax.random.uniform(seed_element_three, (NS,), jnp.float32)
    planted = (place % 16 != 0) & (chance < 0.125)
    prefer = chance < 0.0625
    top_block = ranks[jnp.arange(RECEIVER_GROUPS) // TB_DEV] == group_count - 1
    row_ids = chosen[place // BLOCK]
    raw = jax.random.randint(key_d, (NS, SLOTS), 0, 2 ** 19)
    boost = jnp.where(prefer[:, None] & top_block[row_ids], 2 ** 20, 0)
    slot_scores = (raw + boost) * SLOTS + jnp.arange(SLOTS, dtype=jnp.int32)[None, :]
    pick = jnp.argmax(slot_scores, axis=1).astype(jnp.int32)
    block = jnp.take_along_axis(row_ids, pick[:, None], axis=1)[:, 0]
    offset = jax.random.randint(key_e, (NS,), 0, BLOCK)
    target_index = (block * BLOCK + offset).astype(jnp.int32)
    copied = cells[target_index].astype(jnp.float32) + 0.03 * jax.random.normal(key_f, (NS, EMB), jnp.float32)
    result = jnp.where(planted[:, None], copied, drawn)
    return jnp.clip(result, -2.5, 2.5).astype(jnp.bfloat16)


def steps_of(own_key, dims, cuts, low, high):
    level, own = 1.0, jax.random.fold_in(own_key, 6)
    for axis_at, parts in cuts:
        heights = jnp.exp(jax.random.uniform(jax.random.fold_in(own, axis_at), (parts,), jnp.float32, low / len(cuts), high / len(cuts)))
        level = level * jnp.repeat(heights, dims[axis_at] // parts).reshape([-1 if axis == axis_at else 1 for axis in range(len(dims))])
    return level


def centred(key, shape, deviation, limit, cuts=(), held_as=jnp.bfloat16):
    array = jax.random.normal(key, shape, jnp.float32) * deviation
    if len(cuts) > 0:
        array = steps_of(key, shape, cuts, -0.22, 0.18) * array
    return jnp.clip(array, min=-limit, max=limit).astype(held_as)


def setup_inputs(seed: int = 0) -> dict:
    seeds = jax.random.split(jax.random.key(seed), 7)
    sources = draw_sources(jax.random.fold_in(seeds[6], 71), 0)
    targets = draw_targets(jax.random.fold_in(seeds[6], 71), 0)
    log_src = jnp.clip(-3.0 + 3.0 * jax.random.uniform(seeds[2], (NS,), jnp.float32) ** steps_of(seeds[2], (NS,), ((0, 32),), -0.2, 0.2), -3.0, 0.0)
    log_tgt = jnp.clip(-3.0 + 3.0 * jax.random.uniform(seeds[3], (NT,), jnp.float32) ** steps_of(seeds[3], (NT,), ((0, 4),), -0.2, 0.2), -3.0, 0.0)
    tgt_potential = centred(seeds[4], (NT,), 1.0, 6.0, ((0, 4),), jnp.float32)
    pattern = draw_pattern(jax.random.fold_in(seeds[6], 71), 0)
    return dict(sources=sources, targets=targets, log_src=log_src, log_tgt=log_tgt, tgt_potential=tgt_potential, pattern=pattern)


EPS = 0.05


def reference(sources, targets, log_src, log_tgt, tgt_potential, pattern):
    src_bands = sources.reshape(NBANDS, BLOCK, EMB).astype(jnp.float32)
    tgt_blocks = targets.reshape(RECEIVER_GROUPS, BLOCK, EMB).astype(jnp.float32)
    src_sq = jnp.sum(src_bands * src_bands, axis=-1)
    tgt_sq = jnp.sum(tgt_blocks * tgt_blocks, axis=-1)
    pot_blocks = tgt_potential.reshape(RECEIVER_GROUPS, BLOCK)

    def block_costs(src_band, sq_band, block_ids):
        chosen = tgt_blocks[block_ids]
        inner_prod = jnp.einsum("re,kce->krc", src_band, chosen)
        return sq_band[None, :, None] + tgt_sq[block_ids][:, None, :] - 2.0 * inner_prod

    def row_part(packed):
        src_band, sq_band, block_ids = packed
        segment_ratings = (pot_blocks[block_ids][:, None, :] - block_costs(src_band, sq_band, block_ids)) / EPS
        peak_vals = jnp.max(segment_ratings, axis=(0, 2))
        totals = jnp.sum(jnp.exp(segment_ratings - peak_vals[None, :, None]), axis=(0, 2))
        return peak_vals, totals

    peak_rows, total_rows = lax.map(row_part, (src_bands, src_sq, pattern))
    row_potential = EPS * log_src - EPS * (peak_rows + jnp.log(total_rows)).reshape(-1)
    row_bands = row_potential.reshape(NBANDS, BLOCK)

    def column_step(carry, packed):
        acc_peak, acc_total = carry
        src_band, sq_band, block_ids, band_pot = packed
        segment_ratings = (band_pot[None, :, None] - block_costs(src_band, sq_band, block_ids)) / EPS
        col_peak = jnp.max(segment_ratings, axis=1)
        col_total = jnp.sum(jnp.exp(segment_ratings - col_peak[:, None, :]), axis=1)
        old_peak = acc_peak[block_ids]
        old_total = acc_total[block_ids]
        new_peak = jnp.maximum(old_peak, col_peak)
        new_total = old_total * jnp.exp(old_peak - new_peak) + col_total * jnp.exp(col_peak - new_peak)
        return (acc_peak.at[block_ids].set(new_peak), acc_total.at[block_ids].set(new_total)), None

    start = (jnp.full((RECEIVER_GROUPS, BLOCK), -1e30, jnp.float32), jnp.zeros((RECEIVER_GROUPS, BLOCK), jnp.float32))
    (acc_peak, acc_total), _ = lax.scan(column_step, start, (src_bands, src_sq, pattern, row_bands))
    col_potential = EPS * log_tgt - EPS * (acc_peak + jnp.log(acc_total)).reshape(-1)
    return row_potential, col_potential
```

```python
import functools
import math

import jax
import jax.numpy as jnp
from jax import lax
from jax.experimental import pallas as pl
from jax.experimental.pallas import tpu as pltpu
from jax.sharding import PartitionSpec as P

BLOCK = 256
EPS = 0.05
FLOOR = -1e30
LOG2E = math.log2(math.e)
LN2 = math.log(2.0)
RATE = LOG2E / EPS
GROUP = 8
WIDTH = 256
PAD = 4 * GROUP
VMEM_LIMIT = 56 * 2**20


def three_parts(value):
    first = value.astype(jnp.bfloat16)
    rest = value - first.astype(jnp.float32)
    second = rest.astype(jnp.bfloat16)
    third = (rest - second.astype(jnp.float32)).astype(jnp.bfloat16)
    return first, second, third


def part_rows(row):
    parts = [p.astype(jnp.float32) for p in three_parts(row)]
    at = lax.broadcasted_iota(jnp.int32, (8, row.shape[-1]), 0)
    rows = jnp.zeros((8, row.shape[-1]), jnp.float32)
    for k, part in enumerate(parts):
        rows = jnp.where(at == k, part, rows)
    return rows


def unit_rows(width):
    at = lax.broadcasted_iota(jnp.int32, (8, width), 0)
    return jnp.where(at < 3, 1.0, 0.0).astype(jnp.float32)


def as_columns(first_rows, second_rows):
    width = first_rows.shape[-1]
    tall = jnp.concatenate(
        [
            jnp.zeros((64, width), jnp.float32),
            first_rows,
            second_rows,
            jnp.zeros((48, width), jnp.float32),
        ],
        axis=0,
    )
    return tall.T.astype(jnp.bfloat16)


def square_rows(cells):
    wide = cells.astype(jnp.float32)
    squares = wide * wide
    high = squares.astype(jnp.bfloat16)
    low = (squares - high.astype(jnp.float32)).astype(jnp.bfloat16)
    both = jnp.concatenate([high, low], axis=1)
    ones = jnp.ones((8, both.shape[1]), jnp.bfloat16)
    return lax.dot_general(ones, both, (((1,), (1,)), ((), ())), preferred_element_type=jnp.float32)


def block_rows(index):
    return pl.ds(pl.multiple_of(index * BLOCK, BLOCK), BLOCK)


def running_pairs(count, product, tile_a, tile_b, peak_a, peak_b, peak_ref, total_ref, place):
    def first_stage(pair, tile, peak, slot):
        values = product(pair)
        tile[slot] = values
        peak[slot] = jnp.max(values.reshape(BLOCK // 8, 8, BLOCK), axis=0)

    def second_stage(pair, tile, peak, slot):
        at = place(pair)
        old = peak_ref[at]
        new = jnp.maximum(old, peak[slot])
        peak_ref[at] = new
        shifted = tile[slot].reshape(BLOCK // 8, 8, BLOCK) - new[None]
        total_ref[at] = total_ref[at] * jnp.exp2(old - new) + jnp.sum(jnp.exp2(shifted), axis=0)

    for slot in range(GROUP):
        first_stage(slot, tile_a, peak_a, slot)

    def step(it, carry):
        start = it * (2 * GROUP)
        for slot in range(GROUP):
            first_stage(start + GROUP + slot, tile_b, peak_b, slot)
            second_stage(start + slot, tile_a, peak_a, slot)
        for slot in range(GROUP):
            first_stage(start + 2 * GROUP + slot, tile_a, peak_a, slot)
            second_stage(start + GROUP + slot, tile_b, peak_b, slot)
        return carry

    lax.fori_loop(0, (count + 2 * GROUP - 1) // (2 * GROUP), step, 0)


def finished(peak, total):
    top = jnp.max(peak, axis=1)
    scaled = jnp.sum(total * jnp.exp2(peak - top[:, None, :]), axis=1)
    return top + jnp.log2(jnp.maximum(scaled, 1e-37))


def row_kernel(
    bands, slots, blocks, ids_ref, src_ref, tgt_ref, pot_ref,
    lse_ref, sq_ref, tgt_wide_ref, list_ref, count_ref,
    src_wide_ref, tile_a, tile_b, peak_a, peak_b, peak_ref, total_ref,
):
    lane = lax.broadcasted_iota(jnp.int32, (BLOCK, 128), 1)

    def widen_target(block, carry):
        rows = block_rows(block)
        cells = tgt_ref[rows, :]
        parts = three_parts(cells.astype(jnp.float32) * (2.0 * RATE))
        height = RATE * (pot_ref[pl.ds(block, 1), :] - square_rows(cells))
        extra = as_columns(part_rows(height), unit_rows(BLOCK))
        tgt_wide_ref[rows, 0:128] = jnp.concatenate([parts[0], parts[1]], axis=1)
        last = jnp.concatenate([parts[2], parts[2]], axis=1)
        tgt_wide_ref[rows, 128:256] = jnp.where(lane < 64, last, extra)
        return carry

    lax.fori_loop(0, blocks, widen_target, 0)

    def widen_source(band, count):
        rows = block_rows(band)
        cells = src_ref[rows, :]
        twice = jnp.concatenate([cells, cells], axis=1)
        src_wide_ref[rows, 0:128] = twice
        unit = jnp.where(lane < 67, 1.0, 0.0).astype(jnp.bfloat16)
        src_wide_ref[rows, 128:256] = jnp.where(lane < 64, twice, unit)
        sq_ref[pl.ds(band, 1), :] = square_rows(cells)[0:1, :]
        for slot in range(slots):
            block = ids_ref[band * slots + slot]
            list_ref[count] = band * blocks + block
            mine = jnp.logical_and(block >= 0, block < blocks)
            count = count + jnp.where(mine, 1, 0)
        return count

    count = lax.fori_loop(0, bands, widen_source, jnp.int32(0))
    for k in range(PAD):
        list_ref[count + k] = bands * blocks
    count_ref[0] = count
    peak_ref[...] = jnp.full(peak_ref.shape, FLOOR, jnp.float32)
    total_ref[...] = jnp.zeros(total_ref.shape, jnp.float32)

    def product(pair):
        code = list_ref[pair]
        band = jnp.minimum(code // blocks, bands - 1)
        return lax.dot_general(
            tgt_wide_ref[block_rows(code % blocks), :], src_wide_ref[block_rows(band), :],
            (((1,), (1,)), ((), ())), preferred_element_type=jnp.float32,
        )

    def place(pair):
        return list_ref[pair] // blocks

    running_pairs(count, product, tile_a, tile_b, peak_a, peak_b, peak_ref, total_ref, place)
    lse_ref[...] = finished(peak_ref[0:bands], total_ref[0:bands])


def col_kernel(
    bands, blocks, list_ref, count_ref, src_ref, tgt_wide_ref, pot_ref,
    lse_ref,
    src_wide_ref, tile_a, tile_b, peak_a, peak_b, peak_ref, total_ref,
):
    lane = lax.broadcasted_iota(jnp.int32, (BLOCK, 128), 1)

    def widen_source(band, carry):
        rows = block_rows(band)
        cells = src_ref[rows, :]
        twice = jnp.concatenate([cells, cells], axis=1)
        src_wide_ref[rows, 0:128] = twice
        extra = as_columns(unit_rows(BLOCK), part_rows(pot_ref[pl.ds(band, 1), :]))
        src_wide_ref[rows, 128:256] = jnp.where(lane < 64, twice, extra)
        return carry

    lax.fori_loop(0, bands, widen_source, 0)
    peak_ref[...] = jnp.full(peak_ref.shape, FLOOR, jnp.float32)
    total_ref[...] = jnp.zeros(total_ref.shape, jnp.float32)

    def product(pair):
        code = list_ref[pair]
        band = jnp.minimum(code // blocks, bands - 1)
        return lax.dot_general(
            src_wide_ref[block_rows(band), :], tgt_wide_ref[block_rows(code % blocks), :],
            (((1,), (1,)), ((), ())), preferred_element_type=jnp.float32,
        )

    def place(pair):
        code = list_ref[pair]
        return jnp.where(code >= bands * blocks, blocks, code % blocks)

    running_pairs(count_ref[0], product, tile_a, tile_b, peak_a, peak_b, peak_ref, total_ref, place)
    lse_ref[...] = finished(peak_ref[0:blocks], total_ref[0:blocks])


def joined(values):
    top = functools.reduce(jnp.maximum, values)
    return top + jnp.log2(sum(jnp.exp2(v - top) for v in values))


def turned(value, axis, size, move):
    return lax.ppermute(value, axis, [(k, move(k)) for k in range(size)])


def shards(src_dims, sources, targets, log_src, log_tgt, tgt_potential, pattern):
    bands, slots = pattern.shape
    blocks = targets.shape[0] // BLOCK
    groups = lax.axis_size("tgt")
    ids = (pattern - lax.axis_index("tgt") * blocks).reshape(-1)
    pot_blocks = tgt_potential.reshape(blocks, BLOCK)
    vmem = pl.BlockSpec(memory_space=pltpu.VMEM)
    smem = pl.BlockSpec(memory_space=pltpu.SMEM)
    params = pltpu.CompilerParams(vmem_limit_bytes=VMEM_LIMIT)

    def scratch(places):
        return [
            pltpu.VMEM((bands * BLOCK, WIDTH), jnp.bfloat16),
            pltpu.VMEM((GROUP, BLOCK, BLOCK), jnp.float32),
            pltpu.VMEM((GROUP, BLOCK, BLOCK), jnp.float32),
            pltpu.VMEM((GROUP, 8, BLOCK), jnp.float32),
            pltpu.VMEM((GROUP, 8, BLOCK), jnp.float32),
            pltpu.VMEM((places + 1, 8, BLOCK), jnp.float32),
            pltpu.VMEM((places + 1, 8, BLOCK), jnp.float32),
        ]

    row_lse, src_sq, tgt_wide, pairs, count = pl.pallas_call(
        functools.partial(row_kernel, bands, slots, blocks),
        out_shape=(
            jax.ShapeDtypeStruct((bands, BLOCK), jnp.float32),
            jax.ShapeDtypeStruct((bands, BLOCK), jnp.float32),
            jax.ShapeDtypeStruct((blocks * BLOCK, WIDTH), jnp.bfloat16),
            jax.ShapeDtypeStruct((bands * slots + PAD,), jnp.int32),
            jax.ShapeDtypeStruct((1,), jnp.int32),
        ),
        in_specs=[smem, vmem, vmem, vmem],
        out_specs=(vmem, vmem, vmem, smem, smem),
        scratch_shapes=scratch(bands),
        compiler_params=params,
    )(ids, sources, targets, pot_blocks)

    others = [turned(row_lse, "tgt", groups, lambda k, s=s: (k + s) % groups) for s in range(1, groups)]
    row_all = joined([row_lse] + others)
    log_bands = log_src.reshape(bands, BLOCK)
    row_potential = EPS * log_bands - (EPS * LN2) * row_all + src_sq
    lift = LOG2E * log_bands - row_all

    col_lse = pl.pallas_call(
        functools.partial(col_kernel, bands, blocks),
        out_shape=jax.ShapeDtypeStruct((blocks, BLOCK), jnp.float32),
        in_specs=[smem, smem, vmem, vmem, vmem],
        out_specs=vmem,
        scratch_shapes=scratch(blocks),
        compiler_params=params,
    )(pairs, count, sources, tgt_wide, lift)

    size = lax.axis_size("src")
    stride = size
    for dim in src_dims:
        stride //= dim

        def shifted(k, s, dim=dim, stride=stride):
            here = (k // stride) % dim
            return k + ((here + s) % dim - here) * stride

        col_lse = joined(
            [col_lse] + [turned(col_lse, "src", size, lambda k, s=s: shifted(k, s)) for s in range(1, dim)]
        )
    col_potential = EPS * log_tgt.reshape(blocks, BLOCK) - (EPS * LN2) * col_lse + pot_blocks
    return (row_potential.reshape(-1), col_potential.reshape(-1))


def src_factors(size):
    side = math.isqrt(size // 2)
    return (side, size // 2 // side, 2)


def solution(mesh):
    in_specs = (P("src", None), P("tgt", None), P("src"), P("tgt"), P("tgt"), P("src", None))
    out_specs = (P("src"), P("tgt"))
    body = functools.partial(shards, src_factors(mesh.shape["src"]))
    return jax.shard_map(body, mesh=mesh, in_specs=in_specs, out_specs=out_specs, check_vma=False)
```

```python
import functools
import math

import jax
import jax.numpy as jnp
from jax import lax
from jax.experimental import pallas as pl
from jax.experimental.pallas import tpu as pltpu
from jax.sharding import PartitionSpec as P

BLOCK = 256
EPS = 0.05
FLOOR = -1e30
LOG2E = math.log2(math.e)
LN2 = math.log(2.0)
RATE = LOG2E / EPS
GROUP = 8
UNROLL = 4
WIDTH = 256
PAD = 4 * GROUP
VMEM_LIMIT = 56 * 2**20


def three_parts(value):
    first = value.astype(jnp.bfloat16)
    rest = value - first.astype(jnp.float32)
    second = rest.astype(jnp.bfloat16)
    third = (rest - second.astype(jnp.float32)).astype(jnp.bfloat16)
    return first, second, third


def part_rows(row):
    parts = [p.astype(jnp.float32) for p in three_parts(row)]
    at = lax.broadcasted_iota(jnp.int32, (8, row.shape[-1]), 0)
    rows = jnp.zeros((8, row.shape[-1]), jnp.float32)
    for k, part in enumerate(parts):
        rows = jnp.where(at == k, part, rows)
    return rows


def unit_rows(width):
    at = lax.broadcasted_iota(jnp.int32, (8, width), 0)
    return jnp.where(at < 3, 1.0, 0.0).astype(jnp.float32)


def stacked(first, second, third, first_rows, second_rows):
    extra = jnp.concatenate([first_rows, second_rows], axis=0).astype(jnp.bfloat16)
    blank = jnp.zeros((WIDTH - 208, extra.shape[1]), jnp.bfloat16)
    return jnp.concatenate([first, second, third, extra, blank], axis=0)


def squares(wide):
    return jnp.sum(wide * wide, axis=0, keepdims=True)


def block_rows(index):
    return pl.ds(pl.multiple_of(index * BLOCK, BLOCK), BLOCK)


def running_pairs(count, product, tile_a, tile_b, peak_a, peak_b, peak_ref, total_ref, place):
    def first_stage(pair, tile, peak, slot):
        values = product(pair)
        tile[slot] = values
        peak[slot] = jnp.max(values.reshape(BLOCK // 8, 8, BLOCK), axis=0)

    def second_stage(pair, tile, peak, slot):
        at = place(pair)
        old = peak_ref[at]
        new = jnp.maximum(old, peak[slot])
        peak_ref[at] = new
        shifted = tile[slot].reshape(BLOCK // 8, 8, BLOCK) - new[None]
        total_ref[at] = total_ref[at] * jnp.exp2(old - new) + jnp.sum(jnp.exp2(shifted), axis=0)

    for slot in range(GROUP):
        first_stage(slot, tile_a, peak_a, slot)

    def step(it, carry):
        start = it * (2 * GROUP)
        for slot in range(GROUP):
            first_stage(start + GROUP + slot, tile_b, peak_b, slot)
            second_stage(start + slot, tile_a, peak_a, slot)
        for slot in range(GROUP):
            first_stage(start + 2 * GROUP + slot, tile_a, peak_a, slot)
            second_stage(start + GROUP + slot, tile_b, peak_b, slot)
        return carry

    lax.fori_loop(0, (count + 2 * GROUP - 1) // (2 * GROUP), step, 0)


def finished(peak, total):
    top = jnp.max(peak, axis=1)
    scaled = jnp.sum(total * jnp.exp2(peak - top[:, None, :]), axis=1)
    return top + jnp.log2(jnp.maximum(scaled, 1e-37))


def row_kernel(
    bands, slots, blocks, ids_ref, src_hbm, tgt_hbm, pot_ref,
    lse_ref, sq_ref, tall_hbm, list_ref, count_ref,
    src_ref, tgt_ref, tgt_tall_ref, arrived, tgt_wide_ref, tile_a, tile_b, peak_a, peak_b, peak_ref, total_ref,
):
    unit = unit_rows(BLOCK)
    tgt_copy = pltpu.make_async_copy(tgt_hbm, tgt_ref, arrived.at[0])
    src_copy = pltpu.make_async_copy(src_hbm, src_ref, arrived.at[1])
    tall_copy = pltpu.make_async_copy(tgt_tall_ref, tall_hbm, arrived.at[2])
    tgt_copy.start()
    src_copy.start()

    def widen_target(block):
        wide = tgt_ref[:, block_rows(block)].astype(jnp.float32)
        parts = three_parts(wide * (2.0 * RATE))
        height = RATE * (pot_ref[pl.ds(block, 1), :] - squares(wide))
        tall = stacked(*parts, part_rows(height), unit)
        tgt_tall_ref[block] = tall
        tgt_wide_ref[block] = tall.T

    def list_band(band, count):
        for slot in range(slots):
            code = ids_ref[slot, band]
            list_ref[count] = code
            count = count + 1 + lax.shift_right_arithmetic(code, 31)
        return count

    def list_bands(it, count):
        for k in range(UNROLL):
            count = list_band(it * UNROLL + k, count)
        return count

    count = lax.fori_loop(0, bands // UNROLL, list_bands, jnp.int32(0))
    for k in range(PAD):
        list_ref[count + k] = bands * blocks
    count_ref[0] = count
    peak_ref[...] = jnp.full(peak_ref.shape, FLOOR, jnp.float32)
    total_ref[...] = jnp.zeros(total_ref.shape, jnp.float32)

    def widen(it, carry):
        for k in range(UNROLL):
            widen_target(it * UNROLL + k)
        return carry

    tgt_copy.wait()
    lax.fori_loop(0, blocks // UNROLL, widen, 0)
    tall_copy.start()
    src_copy.wait()

    def norms(it, carry):
        for k in range(UNROLL):
            band = it * UNROLL + k
            sq_ref[pl.ds(band, 1), :] = squares(src_ref[:, block_rows(band)].astype(jnp.float32))
        return carry

    lax.fori_loop(0, bands // UNROLL, norms, 0)

    def product(pair):
        code = list_ref[pair]
        band = jnp.minimum(code // blocks, bands - 1)
        cells = src_ref[:, block_rows(band)]
        tall = stacked(cells, cells, cells, unit, jnp.zeros_like(unit))
        return jnp.dot(tgt_wide_ref[code % blocks], tall, preferred_element_type=jnp.float32)

    def place(pair):
        return list_ref[pair] // blocks

    running_pairs(count, product, tile_a, tile_b, peak_a, peak_b, peak_ref, total_ref, place)
    lse_ref[...] = finished(peak_ref[0:bands], total_ref[0:bands])
    tall_copy.wait()


def col_kernel(
    bands, blocks, list_ref, count_ref, src_hbm, tall_hbm, lift_ref,
    lse_ref,
    src_ref, tgt_tall_ref, arrived, src_wide_ref, tile_a, tile_b, peak_a, peak_b, peak_ref, total_ref,
):
    unit = unit_rows(BLOCK)
    src_copy = pltpu.make_async_copy(src_hbm, src_ref, arrived.at[0])
    tall_copy = pltpu.make_async_copy(tall_hbm, tgt_tall_ref, arrived.at[1])
    src_copy.start()
    tall_copy.start()
    peak_ref[...] = jnp.full(peak_ref.shape, FLOOR, jnp.float32)
    total_ref[...] = jnp.zeros(total_ref.shape, jnp.float32)

    def prepare(it, carry):
        for k in range(UNROLL):
            band = it * UNROLL + k
            cells = src_ref[:, block_rows(band)]
            lift = part_rows(lift_ref[pl.ds(band, 1), :])
            src_wide_ref[band] = stacked(cells, cells, cells, unit, lift).T
        return carry

    src_copy.wait()
    lax.fori_loop(0, bands // UNROLL, prepare, 0)
    tall_copy.wait()

    def product(pair):
        code = list_ref[pair]
        band = jnp.minimum(code // blocks, bands - 1)
        return jnp.dot(src_wide_ref[band], tgt_tall_ref[code % blocks], preferred_element_type=jnp.float32)

    def place(pair):
        code = list_ref[pair]
        return jnp.where(code >= bands * blocks, blocks, code % blocks)

    running_pairs(count_ref[0], product, tile_a, tile_b, peak_a, peak_b, peak_ref, total_ref, place)
    lse_ref[...] = finished(peak_ref[0:blocks], total_ref[0:blocks])


def joined(values):
    top = functools.reduce(jnp.maximum, values)
    return top + jnp.log2(sum(jnp.exp2(v - top) for v in values))


def turned(value, axis, size, move):
    return lax.ppermute(value, axis, [(k, move(k)) for k in range(size)])


def shards(src_dims, sources, targets, log_src, log_tgt, tgt_potential, pattern):
    bands, slots = pattern.shape
    blocks = targets.shape[0] // BLOCK
    groups = lax.axis_size("tgt")
    own = pattern - lax.axis_index("tgt") * blocks
    code = jnp.arange(bands, dtype=jnp.int32)[:, None] * blocks + own
    ids = jnp.where((own >= 0) & (own < blocks), code, -1).T
    pot_blocks = tgt_potential.reshape(blocks, BLOCK)
    vmem = pl.BlockSpec(memory_space=pltpu.VMEM)
    smem = pl.BlockSpec(memory_space=pltpu.SMEM)
    hbm = pl.BlockSpec(memory_space=pl.ANY)
    params = pltpu.CompilerParams(vmem_limit_bytes=VMEM_LIMIT)

    def scratch(wide, places, *extra):
        return [
            pltpu.VMEM(sources.shape[::-1], jnp.bfloat16),
            *extra,
            pltpu.VMEM((blocks, WIDTH, BLOCK), jnp.bfloat16),
            pltpu.SemaphoreType.DMA((3,)),
            pltpu.VMEM((wide, BLOCK, WIDTH), jnp.bfloat16),
            pltpu.VMEM((GROUP, BLOCK, BLOCK), jnp.float32),
            pltpu.VMEM((GROUP, BLOCK, BLOCK), jnp.float32),
            pltpu.VMEM((GROUP, 8, BLOCK), jnp.float32),
            pltpu.VMEM((GROUP, 8, BLOCK), jnp.float32),
            pltpu.VMEM((places + 1, 8, BLOCK), jnp.float32),
            pltpu.VMEM((places + 1, 8, BLOCK), jnp.float32),
        ]

    row_lse, src_sq, tgt_tall, pairs, count = pl.pallas_call(
        functools.partial(row_kernel, bands, slots, blocks),
        out_shape=(
            jax.ShapeDtypeStruct((bands, BLOCK), jnp.float32),
            jax.ShapeDtypeStruct((bands, BLOCK), jnp.float32),
            jax.ShapeDtypeStruct((blocks, WIDTH, BLOCK), jnp.bfloat16),
            jax.ShapeDtypeStruct((bands * slots + PAD,), jnp.int32),
            jax.ShapeDtypeStruct((1,), jnp.int32),
        ),
        in_specs=[smem, hbm, hbm, vmem],
        out_specs=(vmem, vmem, hbm, smem, smem),
        scratch_shapes=scratch(blocks, bands, pltpu.VMEM(targets.shape[::-1], jnp.bfloat16)),
        compiler_params=params,
    )(ids, sources.T, targets.T, pot_blocks)

    others = [turned(row_lse, "tgt", groups, lambda k, s=s: (k + s) % groups) for s in range(1, groups)]
    row_all = joined([row_lse] + others)
    log_bands = log_src.reshape(bands, BLOCK)
    row_potential = EPS * log_bands - (EPS * LN2) * row_all + src_sq
    lift = LOG2E * log_bands - row_all

    col_lse = pl.pallas_call(
        functools.partial(col_kernel, bands, blocks),
        out_shape=jax.ShapeDtypeStruct((blocks, BLOCK), jnp.float32),
        in_specs=[smem, smem, hbm, hbm, vmem],
        out_specs=vmem,
        scratch_shapes=scratch(bands, blocks),
        compiler_params=params,
    )(pairs, count, sources.T, tgt_tall, lift)

    size = lax.axis_size("src")
    stride = size
    for dim in src_dims:
        stride //= dim

        def shifted(k, s, dim=dim, stride=stride):
            here = (k // stride) % dim
            return k + ((here + s) % dim - here) * stride

        col_lse = joined(
            [col_lse] + [turned(col_lse, "src", size, lambda k, s=s: shifted(k, s)) for s in range(1, dim)]
        )
    col_potential = EPS * log_tgt.reshape(blocks, BLOCK) - (EPS * LN2) * col_lse + pot_blocks
    return (row_potential.reshape(-1), col_potential.reshape(-1))


def src_factors(size):
    side = math.isqrt(size // 2)
    return (side, size // 2 // side, 2)


def solution(mesh):
    in_specs = (P("src", None), P("tgt", None), P("src"), P("tgt"), P("tgt"), P("src", None))
    out_specs = (P("src"), P("tgt"))
    body = functools.partial(shards, src_factors(mesh.shape["src"]))
    return jax.shard_map(body, mesh=mesh, in_specs=in_specs, out_specs=out_specs, check_vma=False)
```

```python
import functools
import math

import jax
import jax.numpy as jnp
from jax import lax
from jax.experimental import pallas as pl
from jax.experimental.pallas import tpu as pltpu
from jax.sharding import PartitionSpec as P

BLOCK = 256
EPS = 0.05
FLOOR = -1e30
LOG2E = math.log2(math.e)
LN2 = math.log(2.0)
RATE = LOG2E / EPS
GROUP = 12
UNROLL = 4
WIDTH = 256
PAD = 4 * GROUP
VMEM_LIMIT = 56 * 2**20


def three_parts(value):
    first = value.astype(jnp.bfloat16)
    rest = value - first.astype(jnp.float32)
    second = rest.astype(jnp.bfloat16)
    third = (rest - second.astype(jnp.float32)).astype(jnp.bfloat16)
    return first, second, third


def part_rows(row):
    parts = [p.astype(jnp.float32) for p in three_parts(row)]
    at = lax.broadcasted_iota(jnp.int32, (8, row.shape[-1]), 0)
    rows = jnp.zeros((8, row.shape[-1]), jnp.float32)
    for k, part in enumerate(parts):
        rows = jnp.where(at == k, part, rows)
    return rows


def unit_rows(width):
    at = lax.broadcasted_iota(jnp.int32, (8, width), 0)
    return jnp.where(at < 3, 1.0, 0.0).astype(jnp.float32)


def stacked(first, second, third, first_rows, second_rows):
    extra = jnp.concatenate([first_rows, second_rows], axis=0).astype(jnp.bfloat16)
    blank = jnp.zeros((WIDTH - 208, extra.shape[1]), jnp.bfloat16)
    return jnp.concatenate([first, second, third, extra, blank], axis=0)


def squares(wide):
    return jnp.sum(wide * wide, axis=0, keepdims=True)


def block_rows(index):
    return pl.ds(pl.multiple_of(index * BLOCK, BLOCK), BLOCK)


def running_pairs(count, product, tile_a, tile_b, peak_a, peak_b, peak_ref, total_ref, place):
    def first_stage(pair, tile, peak, slot):
        values = product(pair)
        tile[slot] = values
        peak[slot] = jnp.max(values.reshape(BLOCK // 8, 8, BLOCK), axis=0)

    def second_stage(pair, tile, peak, slot):
        at = place(pair)
        old = peak_ref[at]
        new = jnp.maximum(old, peak[slot])
        peak_ref[at] = new
        total = total_ref[at] * jnp.exp2(old - new)
        for k in range(0, BLOCK, 64):
            shifted = tile[slot, k:k + 64].reshape(8, 8, BLOCK) - new[None]
            total = total + jnp.sum(jnp.exp2(shifted), axis=0)
        total_ref[at] = total

    for slot in range(GROUP):
        first_stage(slot, tile_a, peak_a, slot)

    def step(it, carry):
        start = it * (2 * GROUP)
        for slot in range(GROUP):
            first_stage(start + GROUP + slot, tile_b, peak_b, slot)
            second_stage(start + slot, tile_a, peak_a, slot)
        for slot in range(GROUP):
            first_stage(start + 2 * GROUP + slot, tile_a, peak_a, slot)
            second_stage(start + GROUP + slot, tile_b, peak_b, slot)
        return carry

    lax.fori_loop(0, (count + 2 * GROUP - 1) // (2 * GROUP), step, 0)


def finished(peak, total):
    top = jnp.max(peak, axis=1)
    scaled = jnp.sum(total * jnp.exp2(peak - top[:, None, :]), axis=1)
    return top + jnp.log2(jnp.maximum(scaled, 1e-37))


def joined(values):
    top = functools.reduce(jnp.maximum, values)
    return top + jnp.log2(sum(jnp.exp2(v - top) for v in values))


def row_kernel(
    bands, slots, blocks, ids_ref, src_hbm, tgt_hbm, pot_ref,
    lse_ref, tall_hbm, list_ref, count_ref,
    src_ref, tgt_ref, tgt_tall_ref, arrived, tgt_wide_ref, tile_a, tile_b, peak_a, peak_b, peak_ref, total_ref,
):
    unit = unit_rows(BLOCK)
    tgt_copy = pltpu.make_async_copy(tgt_hbm, tgt_ref, arrived.at[0])
    src_copy = pltpu.make_async_copy(src_hbm, src_ref, arrived.at[1])
    tall_copy = pltpu.make_async_copy(tgt_tall_ref, tall_hbm, arrived.at[2])
    tgt_copy.start()
    src_copy.start()

    def widen_target(block):
        wide = tgt_ref[:, block_rows(block)].astype(jnp.float32)
        parts = three_parts(wide * (2.0 * RATE))
        height = RATE * (pot_ref[block_rows(block)].reshape(1, BLOCK) - squares(wide))
        tall = stacked(*parts, part_rows(height), unit)
        tgt_tall_ref[block] = tall
        tgt_wide_ref[block] = tall.T

    def list_band(band, count):
        for slot in range(slots):
            code = ids_ref[slot, band]
            list_ref[count] = code
            count = count + 1 + lax.shift_right_arithmetic(code, 31)
        return count

    each = bands // blocks * UNROLL

    def prepare(it, count):
        for k in range(UNROLL):
            widen_target(it * UNROLL + k)
        for k in range(each):
            count = list_band(it * each + k, count)
        return count

    peak_ref[...] = jnp.full(peak_ref.shape, FLOOR, jnp.float32)
    total_ref[...] = jnp.zeros(total_ref.shape, jnp.float32)
    tgt_copy.wait()
    count = lax.fori_loop(0, blocks // UNROLL, prepare, jnp.int32(0))
    for k in range(PAD):
        list_ref[count + k] = bands * blocks
    count_ref[0] = count
    tall_copy.start()
    src_copy.wait()

    def product(pair):
        code = list_ref[pair]
        band = jnp.minimum(code // blocks, bands - 1)
        cells = src_ref[:, block_rows(band)]
        tall = stacked(cells, cells, cells, unit, jnp.zeros_like(unit))
        return jnp.dot(tgt_wide_ref[code % blocks], tall, preferred_element_type=jnp.float32)

    def place(pair):
        return list_ref[pair] // blocks

    running_pairs(count, product, tile_a, tile_b, peak_a, peak_b, peak_ref, total_ref, place)
    lse_ref[...] = finished(peak_ref[0:bands], total_ref[0:bands])
    tall_copy.wait()


def col_kernel(
    bands, blocks, groups, list_ref, count_ref, src_hbm, tall_hbm, log_ref, *refs,
):
    row_refs, refs = refs[:groups], refs[groups:]
    (
        lse_ref, row_ref,
        lift_ref, src_ref, tgt_tall_ref, arrived, src_wide_ref, tile_a, tile_b, peak_a, peak_b, peak_ref, total_ref,
    ) = refs
    unit = unit_rows(BLOCK)
    src_copy = pltpu.make_async_copy(src_hbm, src_ref, arrived.at[0])
    tall_copy = pltpu.make_async_copy(tall_hbm, tgt_tall_ref, arrived.at[1])
    src_copy.start()
    tall_copy.start()
    peak_ref[...] = jnp.full(peak_ref.shape, FLOOR, jnp.float32)
    total_ref[...] = jnp.zeros(total_ref.shape, jnp.float32)

    joined_rows = joined([ref[...] for ref in row_refs])
    lift_ref[...] = LOG2E * log_ref[...] - joined_rows
    row_ref[...] = EPS * log_ref[...] - (EPS * LN2) * joined_rows

    def prepare(it, carry):
        for k in range(UNROLL):
            band = it * UNROLL + k
            cells = src_ref[:, block_rows(band)]
            at = pl.ds(band, 1)
            row_ref[at, :] = row_ref[at, :] + squares(cells.astype(jnp.float32))
            lift = part_rows(lift_ref[at, :])
            src_wide_ref[band] = stacked(cells, cells, cells, unit, lift).T
        return carry

    src_copy.wait()
    lax.fori_loop(0, bands // UNROLL, prepare, 0)
    tall_copy.wait()

    def product(pair):
        code = list_ref[pair]
        band = jnp.minimum(code // blocks, bands - 1)
        return jnp.dot(src_wide_ref[band], tgt_tall_ref[code % blocks], preferred_element_type=jnp.float32)

    def place(pair):
        code = list_ref[pair]
        return jnp.where(code >= bands * blocks, blocks, code % blocks)

    running_pairs(count_ref[0], product, tile_a, tile_b, peak_a, peak_b, peak_ref, total_ref, place)
    lse_ref[...] = finished(peak_ref[0:blocks], total_ref[0:blocks])


def turned(value, axis, size, move):
    return lax.ppermute(value, axis, [(k, move(k)) for k in range(size)])


def shards(src_dims, sources, targets, log_src, log_tgt, tgt_potential, pattern):
    bands, slots = pattern.shape
    blocks = targets.shape[0] // BLOCK
    groups = lax.axis_size("tgt")
    own = pattern - lax.axis_index("tgt") * blocks
    code = jnp.arange(bands, dtype=jnp.int32)[:, None] * blocks + own
    ids = jnp.where((own >= 0) & (own < blocks), code, -1).T
    pot_blocks = tgt_potential.reshape(blocks, BLOCK)
    vmem = pl.BlockSpec(memory_space=pltpu.VMEM)
    smem = pl.BlockSpec(memory_space=pltpu.SMEM)
    hbm = pl.BlockSpec(memory_space=pl.ANY)
    params = pltpu.CompilerParams(vmem_limit_bytes=VMEM_LIMIT)

    def scratch(wide, places, *extra):
        return [
            pltpu.VMEM(sources.shape[::-1], jnp.bfloat16),
            *extra,
            pltpu.VMEM((blocks, WIDTH, BLOCK), jnp.bfloat16),
            pltpu.SemaphoreType.DMA((3,)),
            pltpu.VMEM((wide, BLOCK, WIDTH), jnp.bfloat16),
            pltpu.VMEM((GROUP, BLOCK, BLOCK), jnp.float32),
            pltpu.VMEM((GROUP, BLOCK, BLOCK), jnp.float32),
            pltpu.VMEM((GROUP, 8, BLOCK), jnp.float32),
            pltpu.VMEM((GROUP, 8, BLOCK), jnp.float32),
            pltpu.VMEM((places + 1, 8, BLOCK), jnp.float32),
            pltpu.VMEM((places + 1, 8, BLOCK), jnp.float32),
        ]

    row_lse, tgt_tall, pairs, count = pl.pallas_call(
        functools.partial(row_kernel, bands, slots, blocks),
        out_shape=(
            jax.ShapeDtypeStruct((bands, BLOCK), jnp.float32),
            jax.ShapeDtypeStruct((blocks, WIDTH, BLOCK), jnp.bfloat16),
            jax.ShapeDtypeStruct((bands * slots + PAD,), jnp.int32),
            jax.ShapeDtypeStruct((1,), jnp.int32),
        ),
        in_specs=[smem, hbm, hbm, vmem],
        out_specs=(vmem, hbm, smem, smem),
        scratch_shapes=scratch(blocks, bands, pltpu.VMEM(targets.shape[::-1], jnp.bfloat16)),
        compiler_params=params,
    )(ids, sources.T, targets.T, tgt_potential)

    others = [turned(row_lse, "tgt", groups, lambda k, s=s: (k + s) % groups) for s in range(1, groups)]
    col_lse, row_potential = pl.pallas_call(
        functools.partial(col_kernel, bands, blocks, groups),
        out_shape=(
            jax.ShapeDtypeStruct((blocks, BLOCK), jnp.float32),
            jax.ShapeDtypeStruct((bands, BLOCK), jnp.float32),
        ),
        in_specs=[smem, smem, hbm, hbm, vmem] + [vmem] * groups,
        out_specs=(vmem, vmem),
        scratch_shapes=[pltpu.VMEM((bands, BLOCK), jnp.float32)] + scratch(bands, blocks),
        compiler_params=params,
    )(pairs, count, sources.T, tgt_tall, log_src.reshape(bands, BLOCK), row_lse, *others)

    size = lax.axis_size("src")
    stride = size
    for dim in src_dims:
        stride //= dim

        def shifted(k, s, dim=dim, stride=stride):
            here = (k // stride) % dim
            return k + ((here + s) % dim - here) * stride

        col_lse = joined(
            [col_lse] + [turned(col_lse, "src", size, lambda k, s=s: shifted(k, s)) for s in range(1, dim)]
        )
    col_potential = EPS * log_tgt.reshape(blocks, BLOCK) - (EPS * LN2) * col_lse + pot_blocks
    return (row_potential.reshape(-1), col_potential.reshape(-1))


def src_factors(size):
    side = math.isqrt(size // 2)
    return (side, size // 2 // side, 2)


def solution(mesh):
    in_specs = (P("src", None), P("tgt", None), P("src"), P("tgt"), P("tgt"), P("src", None))
    out_specs = (P("src"), P("tgt"))
    body = functools.partial(shards, src_factors(mesh.shape["src"]))
    return jax.shard_map(body, mesh=mesh, in_specs=in_specs, out_specs=out_specs, check_vma=False)
```

```python
import functools
import math

import jax
import jax.numpy as jnp
from jax import lax
from jax.experimental import pallas as pl
from jax.experimental.pallas import tpu as pltpu
from jax.sharding import PartitionSpec as P

BLOCK = 256
EPS = 0.05
FLOOR = -1e30
LOG2E = math.log2(math.e)
LN2 = math.log(2.0)
RATE = LOG2E / EPS
GROUP = 20
UNROLL = 4
WIDTH = 256
PAD = 2 * GROUP
VMEM_LIMIT = 56 * 2**20


def three_parts(value):
    first = value.astype(jnp.bfloat16)
    rest = value - first.astype(jnp.float32)
    second = rest.astype(jnp.bfloat16)
    third = (rest - second.astype(jnp.float32)).astype(jnp.bfloat16)
    return first, second, third


def part_rows(row):
    parts = [p.astype(jnp.float32) for p in three_parts(row)]
    at = lax.broadcasted_iota(jnp.int32, (8, row.shape[-1]), 0)
    rows = jnp.zeros((8, row.shape[-1]), jnp.float32)
    for k, part in enumerate(parts):
        rows = jnp.where(at == k, part, rows)
    return rows


def unit_rows(width):
    at = lax.broadcasted_iota(jnp.int32, (8, width), 0)
    return jnp.where(at < 3, 1.0, 0.0).astype(jnp.float32)


def stacked(first, second, third, first_rows, second_rows):
    extra = jnp.concatenate([first_rows, second_rows], axis=0).astype(jnp.bfloat16)
    blank = jnp.zeros((WIDTH - 208, extra.shape[1]), jnp.bfloat16)
    return jnp.concatenate([first, second, third, extra, blank], axis=0)


def squares(wide):
    return jnp.sum(wide * wide, axis=0, keepdims=True)


def block_rows(index):
    return pl.ds(pl.multiple_of(index * BLOCK, BLOCK), BLOCK)


def running_pairs(count, product, tile, peak, peak_ref, total_ref, place):
    def first_stage(pair, slot):
        values = product(pair)
        tile[slot] = values
        peak[slot] = jnp.max(values.reshape(BLOCK // 8, 8, BLOCK), axis=0)

    def second_stage(pair, slot):
        at = place(pair)
        old = peak_ref[at]
        new = jnp.maximum(old, peak[slot])
        peak_ref[at] = new
        total = total_ref[at] * jnp.exp2(old - new)
        for k in range(0, BLOCK, 64):
            shifted = tile[slot, k:k + 64].reshape(8, 8, BLOCK) - new[None]
            total = total + jnp.sum(jnp.exp2(shifted), axis=0)
        total_ref[at] = total

    for slot in range(GROUP):
        first_stage(slot, slot)

    def step(it, carry):
        start = it * GROUP
        for slot in range(GROUP):
            second_stage(start + slot, slot)
            first_stage(start + GROUP + slot, slot)
        return carry

    lax.fori_loop(0, (count + GROUP - 1) // GROUP, step, 0)


def finished(peak, total):
    top = jnp.max(peak, axis=1)
    scaled = jnp.sum(total * jnp.exp2(peak - top[:, None, :]), axis=1)
    return top + jnp.log2(jnp.maximum(scaled, 1e-37))


def joined(values):
    top = functools.reduce(jnp.maximum, values)
    return top + jnp.log2(sum(jnp.exp2(v - top) for v in values))


def row_kernel(
    bands, slots, blocks, ids_ref, src_hbm, tgt_hbm, pot_ref,
    lse_ref, tall_hbm, list_ref, count_ref,
    src_ref, tgt_ref, tgt_tall_ref, arrived, tgt_wide_ref, tile, peak, peak_ref, total_ref,
):
    unit = unit_rows(BLOCK)
    tgt_copy = pltpu.make_async_copy(tgt_hbm, tgt_ref, arrived.at[0])
    src_copy = pltpu.make_async_copy(src_hbm, src_ref, arrived.at[1])
    tall_copy = pltpu.make_async_copy(tgt_tall_ref, tall_hbm, arrived.at[2])
    tgt_copy.start()
    src_copy.start()

    def widen_target(block):
        wide = tgt_ref[:, block_rows(block)].astype(jnp.float32)
        parts = three_parts(wide * (2.0 * RATE))
        height = RATE * (pot_ref[block_rows(block)].reshape(1, BLOCK) - squares(wide))
        tall = stacked(*parts, part_rows(height), unit)
        tgt_tall_ref[block] = tall
        tgt_wide_ref[block] = tall.T

    def list_band(band, count):
        for slot in range(slots):
            code = ids_ref[slot, band]
            list_ref[count] = code
            count = count + 1 + lax.shift_right_arithmetic(code, 31)
        return count

    each = bands // blocks * UNROLL

    def prepare(it, count):
        for k in range(UNROLL):
            widen_target(it * UNROLL + k)
        for k in range(each):
            count = list_band(it * each + k, count)
        return count

    peak_ref[...] = jnp.full(peak_ref.shape, FLOOR, jnp.float32)
    total_ref[...] = jnp.zeros(total_ref.shape, jnp.float32)
    tgt_copy.wait()
    count = lax.fori_loop(0, blocks // UNROLL, prepare, jnp.int32(0))
    for k in range(PAD):
        list_ref[count + k] = bands * blocks
    count_ref[0] = count
    tall_copy.start()
    src_copy.wait()

    def product(pair):
        code = list_ref[pair]
        band = jnp.minimum(code // blocks, bands - 1)
        cells = src_ref[:, block_rows(band)]
        tall = stacked(cells, cells, cells, unit, jnp.zeros_like(unit))
        return jnp.dot(tgt_wide_ref[code % blocks], tall, preferred_element_type=jnp.float32)

    def place(pair):
        return list_ref[pair] // blocks

    running_pairs(count, product, tile, peak, peak_ref, total_ref, place)
    lse_ref[...] = finished(peak_ref[0:bands], total_ref[0:bands])
    tall_copy.wait()


def col_kernel(
    bands, blocks, groups, list_ref, count_ref, src_hbm, tall_hbm, log_ref, *refs,
):
    row_refs, refs = refs[:groups], refs[groups:]
    (
        lse_ref, row_ref,
        lift_ref, src_ref, tgt_tall_ref, arrived, src_wide_ref, tile, peak, peak_ref, total_ref,
    ) = refs
    unit = unit_rows(BLOCK)
    src_copy = pltpu.make_async_copy(src_hbm, src_ref, arrived.at[0])
    tall_copy = pltpu.make_async_copy(tall_hbm, tgt_tall_ref, arrived.at[1])
    src_copy.start()
    tall_copy.start()
    peak_ref[...] = jnp.full(peak_ref.shape, FLOOR, jnp.float32)
    total_ref[...] = jnp.zeros(total_ref.shape, jnp.float32)

    joined_rows = joined([ref[...] for ref in row_refs])
    lift_ref[...] = LOG2E * log_ref[...] - joined_rows
    row_ref[...] = EPS * log_ref[...] - (EPS * LN2) * joined_rows

    def prepare(it, carry):
        for k in range(UNROLL):
            band = it * UNROLL + k
            cells = src_ref[:, block_rows(band)]
            at = pl.ds(band, 1)
            row_ref[at, :] = row_ref[at, :] + squares(cells.astype(jnp.float32))
            lift = part_rows(lift_ref[at, :])
            src_wide_ref[band] = stacked(cells, cells, cells, unit, lift).T
        return carry

    src_copy.wait()
    lax.fori_loop(0, bands // UNROLL, prepare, 0)
    tall_copy.wait()

    def product(pair):
        code = list_ref[pair]
        band = jnp.minimum(code // blocks, bands - 1)
        return jnp.dot(src_wide_ref[band], tgt_tall_ref[code % blocks], preferred_element_type=jnp.float32)

    def place(pair):
        code = list_ref[pair]
        return jnp.where(code >= bands * blocks, blocks, code % blocks)

    running_pairs(count_ref[0], product, tile, peak, peak_ref, total_ref, place)
    lse_ref[...] = finished(peak_ref[0:blocks], total_ref[0:blocks])


def spread(size):
    return sorted(range(1, size), key=lambda s: (-min(s, size - s), s))


def turned(value, axis, size, move):
    return lax.ppermute(value, axis, [(k, move(k)) for k in range(size)])


def shards(src_dims, sources, targets, log_src, log_tgt, tgt_potential, pattern):
    bands, slots = pattern.shape
    blocks = targets.shape[0] // BLOCK
    groups = lax.axis_size("tgt")
    own = pattern - lax.axis_index("tgt") * blocks
    code = jnp.arange(bands, dtype=jnp.int32)[:, None] * blocks + own
    ids = jnp.where((own >= 0) & (own < blocks), code, -1).T
    pot_blocks = tgt_potential.reshape(blocks, BLOCK)
    vmem = pl.BlockSpec(memory_space=pltpu.VMEM)
    smem = pl.BlockSpec(memory_space=pltpu.SMEM)
    hbm = pl.BlockSpec(memory_space=pl.ANY)
    params = pltpu.CompilerParams(vmem_limit_bytes=VMEM_LIMIT)

    def scratch(wide, places, *extra):
        return [
            pltpu.VMEM(sources.shape[::-1], jnp.bfloat16),
            *extra,
            pltpu.VMEM((blocks, WIDTH, BLOCK), jnp.bfloat16),
            pltpu.SemaphoreType.DMA((3,)),
            pltpu.VMEM((wide, BLOCK, WIDTH), jnp.bfloat16),
            pltpu.VMEM((GROUP, BLOCK, BLOCK), jnp.float32),
            pltpu.VMEM((GROUP, 8, BLOCK), jnp.float32),
            pltpu.VMEM((places + 1, 8, BLOCK), jnp.float32),
            pltpu.VMEM((places + 1, 8, BLOCK), jnp.float32),
        ]

    row_lse, tgt_tall, pairs, count = pl.pallas_call(
        functools.partial(row_kernel, bands, slots, blocks),
        out_shape=(
            jax.ShapeDtypeStruct((bands, BLOCK), jnp.float32),
            jax.ShapeDtypeStruct((blocks, WIDTH, BLOCK), jnp.bfloat16),
            jax.ShapeDtypeStruct((bands * slots + PAD,), jnp.int32),
            jax.ShapeDtypeStruct((1,), jnp.int32),
        ),
        in_specs=[smem, hbm, hbm, vmem],
        out_specs=(vmem, hbm, smem, smem),
        scratch_shapes=scratch(blocks, bands, pltpu.VMEM(targets.shape[::-1], jnp.bfloat16)),
        compiler_params=params,
    )(ids, sources.T, targets.T, tgt_potential)

    others = [turned(row_lse, "tgt", groups, lambda k, s=s: (k + s) % groups) for s in spread(groups)]
    col_lse, row_potential = pl.pallas_call(
        functools.partial(col_kernel, bands, blocks, groups),
        out_shape=(
            jax.ShapeDtypeStruct((blocks, BLOCK), jnp.float32),
            jax.ShapeDtypeStruct((bands, BLOCK), jnp.float32),
        ),
        in_specs=[smem, smem, hbm, hbm, vmem] + [vmem] * groups,
        out_specs=(vmem, vmem),
        scratch_shapes=[pltpu.VMEM((bands, BLOCK), jnp.float32)] + scratch(bands, blocks),
        compiler_params=params,
    )(pairs, count, sources.T, tgt_tall, log_src.reshape(bands, BLOCK), row_lse, *others)

    size = lax.axis_size("src")
    stride = 1
    for dim in reversed(src_dims):

        def shifted(k, s, dim=dim, stride=stride):
            here = (k // stride) % dim
            return k + ((here + s) % dim - here) * stride

        col_lse = joined(
            [col_lse] + [turned(col_lse, "src", size, lambda k, s=s: shifted(k, s)) for s in spread(dim)]
        )
        stride *= dim
    col_potential = EPS * log_tgt.reshape(blocks, BLOCK) - (EPS * LN2) * col_lse + pot_blocks
    return (row_potential.reshape(-1), col_potential.reshape(-1))


def src_factors(size):
    side = math.isqrt(size // 2)
    return (side, size // 2 // side, 2)


def solution(mesh):
    in_specs = (P("src", None), P("tgt", None), P("src"), P("tgt"), P("tgt"), P("src", None))
    out_specs = (P("src"), P("tgt"))
    body = functools.partial(shards, src_factors(mesh.shape["src"]))
    return jax.shard_map(body, mesh=mesh, in_specs=in_specs, out_specs=out_specs, check_vma=False)
```

```python
import functools
import math

import jax
import jax.numpy as jnp
from jax import lax
from jax.experimental import pallas as pl
from jax.experimental.pallas import tpu as pltpu
from jax.sharding import PartitionSpec as P

BLOCK = 256
EPS = 0.05
FLOOR = -1e30
LOG2E = math.log2(math.e)
LN2 = math.log(2.0)
RATE = LOG2E / EPS
GROUP = 24
UNROLL = 4
WIDTH = 256
PAD = 2 * GROUP
VMEM_LIMIT = 56 * 2**20


def three_parts(value):
    first = value.astype(jnp.bfloat16)
    rest = value - first.astype(jnp.float32)
    second = rest.astype(jnp.bfloat16)
    third = (rest - second.astype(jnp.float32)).astype(jnp.bfloat16)
    return first, second, third


def part_rows(row):
    parts = [p.astype(jnp.float32) for p in three_parts(row)]
    at = lax.broadcasted_iota(jnp.int32, (8, row.shape[-1]), 0)
    rows = jnp.zeros((8, row.shape[-1]), jnp.float32)
    for k, part in enumerate(parts):
        rows = jnp.where(at == k, part, rows)
    return rows


def unit_rows(width):
    at = lax.broadcasted_iota(jnp.int32, (8, width), 0)
    return jnp.where(at < 3, 1.0, 0.0).astype(jnp.float32)


def stacked(first, second, third, first_rows, second_rows):
    extra = jnp.concatenate([first_rows, second_rows], axis=0).astype(jnp.bfloat16)
    blank = jnp.zeros((WIDTH - 208, extra.shape[1]), jnp.bfloat16)
    return jnp.concatenate([first, second, third, extra, blank], axis=0)


def squares(wide):
    return jnp.sum(wide * wide, axis=0, keepdims=True)


def block_rows(index):
    return pl.ds(pl.multiple_of(index * BLOCK, BLOCK), BLOCK)


def running_pairs(count, product, tile, peak, peak_ref, total_ref, place):
    def first_stage(pair, slot):
        values = product(pair)
        tile[slot] = values
        peak[slot] = jnp.max(values.reshape(BLOCK // 8, 8, BLOCK), axis=0)

    def second_stage(pair, slot):
        at = place(pair)
        old = peak_ref[at]
        new = jnp.maximum(old, peak[slot])
        peak_ref[at] = new
        scale = jnp.exp2(old - new)
        total = 0.0
        for k in range(0, BLOCK, 64):
            shifted = tile[slot, k:k + 64].reshape(8, 8, BLOCK) - new[None]
            total = total + jnp.sum(jnp.exp2(shifted), axis=0)
        total_ref[at] = total_ref[at] * scale + total

    for slot in range(GROUP):
        first_stage(slot, slot)

    def step(it, carry):
        start = it * GROUP
        for slot in range(GROUP):
            second_stage(start + slot, slot)
            first_stage(start + GROUP + slot, slot)
        return carry

    lax.fori_loop(0, (count + GROUP - 1) // GROUP, step, 0)


def finished(peak, total):
    top = jnp.max(peak, axis=1)
    scaled = jnp.sum(total * jnp.exp2(peak - top[:, None, :]), axis=1)
    return top + jnp.log2(jnp.maximum(scaled, 1e-37))


def joined(values):
    top = functools.reduce(jnp.maximum, values)
    return top + jnp.log2(sum(jnp.exp2(v - top) for v in values))


def row_kernel(
    bands, slots, blocks, ids_ref, src_hbm, tgt_hbm, pot_ref,
    lse_ref, tall_hbm, list_ref, count_ref,
    src_ref, tgt_ref, tgt_tall_ref, arrived, tgt_wide_ref, tile, peak, peak_ref, total_ref,
):
    unit = unit_rows(BLOCK)
    tgt_copy = pltpu.make_async_copy(tgt_hbm, tgt_ref, arrived.at[0])
    src_copy = pltpu.make_async_copy(src_hbm, src_ref, arrived.at[1])
    tall_copy = pltpu.make_async_copy(tgt_tall_ref, tall_hbm, arrived.at[2])
    tgt_copy.start()
    src_copy.start()

    def widen_target(block):
        wide = tgt_ref[:, block_rows(block)].astype(jnp.float32)
        parts = three_parts(wide * (2.0 * RATE))
        height = RATE * (pot_ref[block_rows(block)].reshape(1, BLOCK) - squares(wide))
        tall = stacked(*parts, part_rows(height), unit)
        tgt_tall_ref[block] = tall
        tgt_wide_ref[block] = tall.T

    def list_band(band, count):
        for slot in range(slots):
            code = ids_ref[slot, band]
            list_ref[count] = code
            count = count + 1 + lax.shift_right_arithmetic(code, 31)
        return count

    each = bands // blocks * UNROLL

    def prepare(it, count):
        for k in range(UNROLL):
            widen_target(it * UNROLL + k)
        for k in range(each):
            count = list_band(it * each + k, count)
        return count

    peak_ref[...] = jnp.full(peak_ref.shape, FLOOR, jnp.float32)
    total_ref[...] = jnp.zeros(total_ref.shape, jnp.float32)
    tgt_copy.wait()
    count = lax.fori_loop(0, blocks // UNROLL, prepare, jnp.int32(0))
    for k in range(PAD):
        list_ref[count + k] = bands * blocks
    count_ref[0] = count
    tall_copy.start()
    src_copy.wait()

    def product(pair):
        code = list_ref[pair]
        band = jnp.minimum(code // blocks, bands - 1)
        cells = src_ref[:, block_rows(band)]
        tall = stacked(cells, cells, cells, unit, jnp.zeros_like(unit))
        return jnp.dot(tgt_wide_ref[code % blocks], tall, preferred_element_type=jnp.float32)

    def place(pair):
        return list_ref[pair] // blocks

    running_pairs(count, product, tile, peak, peak_ref, total_ref, place)
    lse_ref[...] = finished(peak_ref[0:bands], total_ref[0:bands])
    tall_copy.wait()


def col_kernel(
    bands, blocks, groups, list_ref, count_ref, src_hbm, tall_hbm, log_ref, *refs,
):
    row_refs, refs = refs[:groups], refs[groups:]
    (
        lse_ref, row_ref,
        lift_ref, src_ref, tgt_tall_ref, arrived, src_wide_ref, tile, peak, peak_ref, total_ref,
    ) = refs
    unit = unit_rows(BLOCK)
    src_copy = pltpu.make_async_copy(src_hbm, src_ref, arrived.at[0])
    tall_copy = pltpu.make_async_copy(tall_hbm, tgt_tall_ref, arrived.at[1])
    src_copy.start()
    tall_copy.start()
    peak_ref[...] = jnp.full(peak_ref.shape, FLOOR, jnp.float32)
    total_ref[...] = jnp.zeros(total_ref.shape, jnp.float32)

    joined_rows = joined([ref[...] for ref in row_refs])
    lift_ref[...] = LOG2E * log_ref[...] - joined_rows
    row_ref[...] = EPS * log_ref[...] - (EPS * LN2) * joined_rows

    def prepare(it, carry):
        for k in range(UNROLL):
            band = it * UNROLL + k
            cells = src_ref[:, block_rows(band)]
            at = pl.ds(band, 1)
            row_ref[at, :] = row_ref[at, :] + squares(cells.astype(jnp.float32))
            lift = part_rows(lift_ref[at, :])
            src_wide_ref[band] = stacked(cells, cells, cells, unit, lift).T
        return carry

    src_copy.wait()
    lax.fori_loop(0, bands // UNROLL, prepare, 0)
    tall_copy.wait()

    def product(pair):
        code = list_ref[pair]
        band = jnp.minimum(code // blocks, bands - 1)
        return jnp.dot(src_wide_ref[band], tgt_tall_ref[code % blocks], preferred_element_type=jnp.float32)

    def place(pair):
        code = list_ref[pair]
        return jnp.where(code >= bands * blocks, blocks, code % blocks)

    running_pairs(count_ref[0], product, tile, peak, peak_ref, total_ref, place)
    lse_ref[...] = finished(peak_ref[0:blocks], total_ref[0:blocks])


def spread(size):
    return sorted(range(1, size), key=lambda s: (-min(s, size - s), s))


def turned(value, axis, size, move):
    return lax.ppermute(value, axis, [(k, move(k)) for k in range(size)])


def shards(src_dims, sources, targets, log_src, log_tgt, tgt_potential, pattern):
    bands, slots = pattern.shape
    blocks = targets.shape[0] // BLOCK
    groups = lax.axis_size("tgt")
    own = pattern - lax.axis_index("tgt") * blocks
    code = jnp.arange(bands, dtype=jnp.int32)[:, None] * blocks + own
    ids = jnp.where((own >= 0) & (own < blocks), code, -1).T
    pot_blocks = tgt_potential.reshape(blocks, BLOCK)
    vmem = pl.BlockSpec(memory_space=pltpu.VMEM)
    smem = pl.BlockSpec(memory_space=pltpu.SMEM)
    hbm = pl.BlockSpec(memory_space=pl.ANY)
    params = pltpu.CompilerParams(vmem_limit_bytes=VMEM_LIMIT)

    def scratch(wide, places, *extra):
        return [
            pltpu.VMEM(sources.shape[::-1], jnp.bfloat16),
            *extra,
            pltpu.VMEM((blocks, WIDTH, BLOCK), jnp.bfloat16),
            pltpu.SemaphoreType.DMA((3,)),
            pltpu.VMEM((wide, BLOCK, WIDTH), jnp.bfloat16),
            pltpu.VMEM((GROUP, BLOCK, BLOCK), jnp.float32),
            pltpu.VMEM((GROUP, 8, BLOCK), jnp.float32),
            pltpu.VMEM((places + 1, 8, BLOCK), jnp.float32),
            pltpu.VMEM((places + 1, 8, BLOCK), jnp.float32),
        ]

    row_lse, tgt_tall, pairs, count = pl.pallas_call(
        functools.partial(row_kernel, bands, slots, blocks),
        out_shape=(
            jax.ShapeDtypeStruct((bands, BLOCK), jnp.float32),
            jax.ShapeDtypeStruct((blocks, WIDTH, BLOCK), jnp.bfloat16),
            jax.ShapeDtypeStruct((bands * slots + PAD,), jnp.int32),
            jax.ShapeDtypeStruct((1,), jnp.int32),
        ),
        in_specs=[smem, hbm, hbm, vmem],
        out_specs=(vmem, hbm, smem, smem),
        scratch_shapes=scratch(blocks, bands, pltpu.VMEM(targets.shape[::-1], jnp.bfloat16)),
        compiler_params=params,
    )(ids, sources.T, targets.T, tgt_potential)

    others = [turned(row_lse, "tgt", groups, lambda k, s=s: (k + s) % groups) for s in spread(groups)]
    col_lse, row_potential = pl.pallas_call(
        functools.partial(col_kernel, bands, blocks, groups),
        out_shape=(
            jax.ShapeDtypeStruct((blocks, BLOCK), jnp.float32),
            jax.ShapeDtypeStruct((bands, BLOCK), jnp.float32),
        ),
        in_specs=[smem, smem, hbm, hbm, vmem] + [vmem] * groups,
        out_specs=(vmem, vmem),
        scratch_shapes=[pltpu.VMEM((bands, BLOCK), jnp.float32)] + scratch(bands, blocks),
        compiler_params=params,
    )(pairs, count, sources.T, tgt_tall, log_src.reshape(bands, BLOCK), row_lse, *others)

    size = lax.axis_size("src")
    stride = 1
    for dim in reversed(src_dims):

        def shifted(k, s, dim=dim, stride=stride):
            here = (k // stride) % dim
            return k + ((here + s) % dim - here) * stride

        col_lse = joined(
            [col_lse] + [turned(col_lse, "src", size, lambda k, s=s: shifted(k, s)) for s in spread(dim)]
        )
        stride *= dim
    col_potential = EPS * log_tgt.reshape(blocks, BLOCK) - (EPS * LN2) * col_lse + pot_blocks
    return (row_potential.reshape(-1), col_potential.reshape(-1))


def src_factors(size):
    side = math.isqrt(size // 2)
    return (side, size // 2 // side, 2)


def solution(mesh):
    in_specs = (P("src", None), P("tgt", None), P("src"), P("tgt"), P("tgt"), P("src", None))
    out_specs = (P("src"), P("tgt"))
    body = functools.partial(shards, src_factors(mesh.shape["src"]))
    return jax.shard_map(body, mesh=mesh, in_specs=in_specs, out_specs=out_specs, check_vma=False)
```

```python
import functools
import math

import jax
import jax.numpy as jnp
from jax import lax
from jax.experimental import pallas as pl
from jax.experimental.pallas import tpu as pltpu
from jax.sharding import PartitionSpec as P

BLOCK = 256
EPS = 0.05
FLOOR = -1e30
LOG2E = math.log2(math.e)
LN2 = math.log(2.0)
RATE = LOG2E / EPS
GROUP = 24
UNROLL = 4
WIDTH = 256
PAD = 2 * GROUP
VMEM_LIMIT = 56 * 2**20


def three_parts(value):
    first = value.astype(jnp.bfloat16)
    rest = value - first.astype(jnp.float32)
    second = rest.astype(jnp.bfloat16)
    third = (rest - second.astype(jnp.float32)).astype(jnp.bfloat16)
    return first, second, third


def part_rows(row):
    parts = [p.astype(jnp.float32) for p in three_parts(row)]
    at = lax.broadcasted_iota(jnp.int32, (8, row.shape[-1]), 0)
    rows = jnp.zeros((8, row.shape[-1]), jnp.float32)
    for k, part in enumerate(parts):
        rows = jnp.where(at == k, part, rows)
    return rows


def unit_rows(width):
    at = lax.broadcasted_iota(jnp.int32, (8, width), 0)
    return jnp.where(at < 3, 1.0, 0.0).astype(jnp.float32)


def stacked(first, second, third, first_rows, second_rows):
    extra = jnp.concatenate([first_rows, second_rows], axis=0).astype(jnp.bfloat16)
    blank = jnp.zeros((WIDTH - 208, extra.shape[1]), jnp.bfloat16)
    return jnp.concatenate([first, second, third, extra, blank], axis=0)


def squares(wide):
    return jnp.sum(wide * wide, axis=0, keepdims=True)


def block_rows(index):
    return pl.ds(pl.multiple_of(index * BLOCK, BLOCK), BLOCK)


def running_pairs(count, product, tile, peak, peak_ref, total_ref, place):
    def first_stage(pair, slot):
        values = product(pair)
        tile[slot] = values
        peak[slot] = jnp.max(values.reshape(BLOCK // 8, 8, BLOCK), axis=0)

    def second_stage(pair, slot):
        at = place(pair)
        old = peak_ref[at]
        new = jnp.maximum(old, peak[slot])
        peak_ref[at] = new
        scale = jnp.exp2(old - new)
        total = 0.0
        for k in range(0, BLOCK, 64):
            shifted = tile[slot, k:k + 64].reshape(8, 8, BLOCK) - new[None]
            total = total + jnp.sum(jnp.exp2(shifted), axis=0)
        total_ref[at] = total_ref[at] * scale + total

    for slot in range(GROUP):
        first_stage(slot, slot)

    def step(it, carry):
        start = it * GROUP
        for slot in range(GROUP):
            second_stage(start + slot, slot)
            first_stage(start + GROUP + slot, slot)
        return carry

    lax.fori_loop(0, (count + GROUP - 1) // GROUP, step, 0)


def finished(peak, total):
    top = jnp.max(peak, axis=1)
    scaled = jnp.sum(total * jnp.exp2(peak - top[:, None, :]), axis=1)
    return top + jnp.log2(jnp.maximum(scaled, 1e-37))


def joined(values):
    top = functools.reduce(jnp.maximum, values)
    return top + jnp.log2(sum(jnp.exp2(v - top) for v in values))


def row_kernel(
    bands, slots, blocks, ids_ref, src_hbm, tgt_hbm, pot_ref,
    lse_ref, tall_hbm, list_ref, count_ref,
    src_ref, tgt_ref, tgt_tall_ref, arrived, tgt_wide_ref, tile, peak, peak_ref, total_ref,
):
    unit = unit_rows(BLOCK)
    tgt_copy = pltpu.make_async_copy(tgt_hbm, tgt_ref, arrived.at[0])
    src_copy = pltpu.make_async_copy(src_hbm, src_ref, arrived.at[1])
    tall_copy = pltpu.make_async_copy(tgt_tall_ref, tall_hbm, arrived.at[2])
    tgt_copy.start()
    src_copy.start()

    def widen_target(block):
        wide = tgt_ref[:, block_rows(block)].astype(jnp.float32)
        parts = three_parts(wide * (2.0 * RATE))
        height = RATE * (pot_ref[block_rows(block)].reshape(1, BLOCK) - squares(wide))
        tall = stacked(*parts, part_rows(height), unit)
        tgt_tall_ref[block] = tall
        tgt_wide_ref[block] = tall.T

    def list_band(band, count):
        for slot in range(slots):
            code = ids_ref[slot, band]
            list_ref[count] = code
            count = count + 1 + lax.shift_right_arithmetic(code, 31)
        return count

    each = bands // blocks * UNROLL

    def prepare(it, count):
        for k in range(UNROLL):
            widen_target(it * UNROLL + k)
        for k in range(each):
            count = list_band(it * each + k, count)
        return count

    peak_ref[...] = jnp.full(peak_ref.shape, FLOOR, jnp.float32)
    total_ref[...] = jnp.zeros(total_ref.shape, jnp.float32)
    tgt_copy.wait()
    count = lax.fori_loop(0, blocks // UNROLL, prepare, jnp.int32(0))
    for k in range(PAD):
        list_ref[count + k] = bands * blocks
    count_ref[0] = count
    tall_copy.start()
    src_copy.wait()

    def product(pair):
        code = list_ref[pair]
        band = jnp.minimum(code // blocks, bands - 1)
        cells = src_ref[:, block_rows(band)]
        tall = stacked(cells, cells, cells, unit, jnp.zeros_like(unit))
        return jnp.dot(tgt_wide_ref[code % blocks], tall, preferred_element_type=jnp.float32)

    def place(pair):
        return list_ref[pair] // blocks

    running_pairs(count, product, tile, peak, peak_ref, total_ref, place)
    lse_ref[...] = finished(peak_ref[0:bands], total_ref[0:bands])
    tall_copy.wait()


def col_kernel(
    bands, blocks, groups, list_ref, count_ref, src_hbm, tall_hbm, log_ref, *refs,
):
    row_refs, refs = refs[:groups], refs[groups:]
    (
        lse_ref, row_ref,
        lift_ref, src_ref, tgt_tall_ref, arrived, src_wide_ref, tile, peak, peak_ref, total_ref,
    ) = refs
    unit = unit_rows(BLOCK)
    src_copy = pltpu.make_async_copy(src_hbm, src_ref, arrived.at[0])
    tall_copy = pltpu.make_async_copy(tall_hbm, tgt_tall_ref, arrived.at[1])
    src_copy.start()
    tall_copy.start()
    peak_ref[...] = jnp.full(peak_ref.shape, FLOOR, jnp.float32)
    total_ref[...] = jnp.zeros(total_ref.shape, jnp.float32)

    joined_rows = joined([ref[...] for ref in row_refs])
    lift_ref[...] = LOG2E * log_ref[...] - joined_rows

    def prepare(it, carry):
        for k in range(UNROLL):
            band = it * UNROLL + k
            cells = src_ref[:, block_rows(band)]
            at = pl.ds(band, 1)
            lift_row = lift_ref[at, :]
            row = (EPS * LN2) * lift_row + squares(cells.astype(jnp.float32))
            row_ref[block_rows(band)] = row.reshape(BLOCK)
            lift = part_rows(lift_row)
            src_wide_ref[band] = stacked(cells, cells, cells, unit, lift).T
        return carry

    src_copy.wait()
    lax.fori_loop(0, bands // UNROLL, prepare, 0)
    tall_copy.wait()

    def product(pair):
        code = list_ref[pair]
        band = jnp.minimum(code // blocks, bands - 1)
        return jnp.dot(src_wide_ref[band], tgt_tall_ref[code % blocks], preferred_element_type=jnp.float32)

    def place(pair):
        code = list_ref[pair]
        return jnp.where(code >= bands * blocks, blocks, code % blocks)

    running_pairs(count_ref[0], product, tile, peak, peak_ref, total_ref, place)
    lse_ref[...] = finished(peak_ref[0:blocks], total_ref[0:blocks])


def spread(size):
    return sorted(range(1, size), key=lambda s: (-min(s, size - s), s))


def turned(value, axis, size, move):
    return lax.ppermute(value, axis, [(k, move(k)) for k in range(size)])


def shards(src_dims, sources, targets, log_src, log_tgt, tgt_potential, pattern):
    bands, slots = pattern.shape
    blocks = targets.shape[0] // BLOCK
    groups = lax.axis_size("tgt")
    own = pattern - lax.axis_index("tgt") * blocks
    code = jnp.arange(bands, dtype=jnp.int32)[:, None] * blocks + own
    ids = jnp.where((own >= 0) & (own < blocks), code, -1).T
    pot_blocks = tgt_potential.reshape(blocks, BLOCK)
    vmem = pl.BlockSpec(memory_space=pltpu.VMEM)
    smem = pl.BlockSpec(memory_space=pltpu.SMEM)
    hbm = pl.BlockSpec(memory_space=pl.ANY)
    params = pltpu.CompilerParams(vmem_limit_bytes=VMEM_LIMIT)

    def scratch(wide, places, *extra):
        return [
            pltpu.VMEM(sources.shape[::-1], jnp.bfloat16),
            *extra,
            pltpu.VMEM((blocks, WIDTH, BLOCK), jnp.bfloat16),
            pltpu.SemaphoreType.DMA((3,)),
            pltpu.VMEM((wide, BLOCK, WIDTH), jnp.bfloat16),
            pltpu.VMEM((GROUP, BLOCK, BLOCK), jnp.float32),
            pltpu.VMEM((GROUP, 8, BLOCK), jnp.float32),
            pltpu.VMEM((places + 1, 8, BLOCK), jnp.float32),
            pltpu.VMEM((places + 1, 8, BLOCK), jnp.float32),
        ]

    row_lse, tgt_tall, pairs, count = pl.pallas_call(
        functools.partial(row_kernel, bands, slots, blocks),
        out_shape=(
            jax.ShapeDtypeStruct((bands, BLOCK), jnp.float32),
            jax.ShapeDtypeStruct((blocks, WIDTH, BLOCK), jnp.bfloat16),
            jax.ShapeDtypeStruct((bands * slots + PAD,), jnp.int32),
            jax.ShapeDtypeStruct((1,), jnp.int32),
        ),
        in_specs=[smem, hbm, hbm, vmem],
        out_specs=(vmem, hbm, smem, smem),
        scratch_shapes=scratch(blocks, bands, pltpu.VMEM(targets.shape[::-1], jnp.bfloat16)),
        compiler_params=params,
    )(ids, sources.T, targets.T, tgt_potential)

    others = [turned(row_lse, "tgt", groups, lambda k, s=s: (k + s) % groups) for s in spread(groups)]
    col_lse, row_potential = pl.pallas_call(
        functools.partial(col_kernel, bands, blocks, groups),
        out_shape=(
            jax.ShapeDtypeStruct((blocks, BLOCK), jnp.float32),
            jax.ShapeDtypeStruct((bands * BLOCK,), jnp.float32),
        ),
        in_specs=[smem, smem, hbm, hbm, vmem] + [vmem] * groups,
        out_specs=(vmem, vmem),
        scratch_shapes=[pltpu.VMEM((bands, BLOCK), jnp.float32)] + scratch(bands, blocks),
        compiler_params=params,
    )(pairs, count, sources.T, tgt_tall, log_src.reshape(bands, BLOCK), row_lse, *others)

    size = lax.axis_size("src")
    stride = 1
    for dim in reversed(src_dims):

        def shifted(k, s, dim=dim, stride=stride):
            here = (k // stride) % dim
            return k + ((here + s) % dim - here) * stride

        col_lse = joined(
            [col_lse] + [turned(col_lse, "src", size, lambda k, s=s: shifted(k, s)) for s in spread(dim)]
        )
        stride *= dim
    col_potential = EPS * log_tgt.reshape(blocks, BLOCK) - (EPS * LN2) * col_lse + pot_blocks
    return (row_potential, col_potential.reshape(-1))


def src_factors(size):
    side = math.isqrt(size // 2)
    return (side, size // 2 // side, 2)


def solution(mesh):
    in_specs = (P("src", None), P("tgt", None), P("src"), P("tgt"), P("tgt"), P("src", None))
    out_specs = (P("src"), P("tgt"))
    body = functools.partial(shards, src_factors(mesh.shape["src"]))
    return jax.shard_map(body, mesh=mesh, in_specs=in_specs, out_specs=out_specs, check_vma=False)
```

```python
import functools
import math

import jax
import jax.numpy as jnp
from jax import lax
from jax.experimental import pallas as pl
from jax.experimental.pallas import tpu as pltpu
from jax.sharding import PartitionSpec as P

BLOCK = 256
EPS = 0.05
FLOOR = -1e30
LOG2E = math.log2(math.e)
LN2 = math.log(2.0)
RATE = LOG2E / EPS
GROUP = 24
UNROLL = 4
WIDTH = 256
PAD = 2 * GROUP
VMEM_LIMIT = 56 * 2**20


def three_parts(value):
    first = value.astype(jnp.bfloat16)
    rest = value - first.astype(jnp.float32)
    second = rest.astype(jnp.bfloat16)
    third = (rest - second.astype(jnp.float32)).astype(jnp.bfloat16)
    return first, second, third


def part_rows(row):
    parts = [p.astype(jnp.float32) for p in three_parts(row)]
    at = lax.broadcasted_iota(jnp.int32, (8, row.shape[-1]), 0)
    rows = jnp.zeros((8, row.shape[-1]), jnp.float32)
    for k, part in enumerate(parts):
        rows = jnp.where(at == k, part, rows)
    return rows


def unit_rows(width):
    at = lax.broadcasted_iota(jnp.int32, (8, width), 0)
    return jnp.where(at < 3, 1.0, 0.0).astype(jnp.float32)


def stacked(first, second, third, first_rows, second_rows):
    extra = jnp.concatenate([first_rows, second_rows], axis=0).astype(jnp.bfloat16)
    blank = jnp.zeros((WIDTH - 208, extra.shape[1]), jnp.bfloat16)
    return jnp.concatenate([first, second, third, extra, blank], axis=0)


def squares(wide):
    return jnp.sum(wide * wide, axis=0, keepdims=True)


def block_rows(index):
    return pl.ds(pl.multiple_of(index * BLOCK, BLOCK), BLOCK)


def running_pairs(count, product, tile, peak, peak_ref, total_ref, place):
    def first_stage(pair, slot):
        values = product(pair)
        tile[slot] = values
        peak[slot] = jnp.max(values.reshape(BLOCK // 8, 8, BLOCK), axis=0)

    def second_stage(pair, slot):
        at = place(pair)
        old = peak_ref[at]
        new = jnp.maximum(old, peak[slot])
        peak_ref[at] = new
        scale = jnp.exp2(old - new)
        total = 0.0
        for k in range(0, BLOCK, 64):
            shifted = tile[slot, k:k + 64].reshape(8, 8, BLOCK) - new[None]
            total = total + jnp.sum(jnp.exp2(shifted), axis=0)
        total_ref[at] = total_ref[at] * scale + total

    for slot in range(GROUP):
        first_stage(slot, slot)

    def step(it, carry):
        start = it * GROUP
        for slot in range(GROUP):
            second_stage(start + slot, slot)
            first_stage(start + GROUP + slot, slot)
        return carry

    lax.fori_loop(0, (count + GROUP - 1) // GROUP, step, 0)


def finished(peak, total):
    top = jnp.max(peak, axis=1)
    scaled = jnp.sum(total * jnp.exp2(peak - top[:, None, :]), axis=1)
    return top + jnp.log2(jnp.maximum(scaled, 1e-37))


def joined(values):
    top = functools.reduce(jnp.maximum, values)
    return top + jnp.log2(sum(jnp.exp2(v - top) for v in values))


def row_kernel(
    bands, slots, blocks, ids_ref, src_hbm, tgt_hbm, pot_ref,
    lse_ref, tall_hbm, list_ref, count_ref,
    src_ref, tgt_ref, tgt_tall_ref, arrived, tgt_wide_ref, tile, peak, peak_ref, total_ref,
):
    unit = unit_rows(BLOCK)
    tgt_copy = pltpu.make_async_copy(tgt_hbm, tgt_ref, arrived.at[0])
    src_copy = pltpu.make_async_copy(src_hbm, src_ref, arrived.at[1])
    tall_copy = pltpu.make_async_copy(tgt_tall_ref, tall_hbm, arrived.at[2])
    tgt_copy.start()
    src_copy.start()

    def widen_target(block):
        wide = tgt_ref[:, block_rows(block)].astype(jnp.float32)
        parts = three_parts(wide * (2.0 * RATE))
        height = RATE * (pot_ref[block_rows(block)].reshape(1, BLOCK) - squares(wide))
        tall = stacked(*parts, part_rows(height), unit)
        tgt_tall_ref[block] = tall
        tgt_wide_ref[block] = tall.T

    def list_band(band, count):
        for slot in range(slots):
            code = ids_ref[slot, band]
            list_ref[count] = code
            count = count + 1 + lax.shift_right_arithmetic(code, 31)
        return count

    each = bands // blocks * UNROLL

    def prepare(it, count):
        for k in range(UNROLL):
            widen_target(it * UNROLL + k)
        for k in range(each):
            count = list_band(it * each + k, count)
        return count

    peak_ref[...] = jnp.full(peak_ref.shape, FLOOR, jnp.float32)
    total_ref[...] = jnp.zeros(total_ref.shape, jnp.float32)
    tgt_copy.wait()
    count = lax.fori_loop(0, blocks // UNROLL, prepare, jnp.int32(0))
    for k in range(PAD):
        list_ref[count + k] = bands * blocks
    count_ref[0] = count
    tall_copy.start()
    src_copy.wait()

    def product(pair):
        code = list_ref[pair]
        band = jnp.minimum(code // blocks, bands - 1)
        cells = src_ref[:, block_rows(band)]
        tall = stacked(cells, cells, cells, unit, jnp.zeros_like(unit))
        return jnp.dot(tgt_wide_ref[code % blocks], tall, preferred_element_type=jnp.float32)

    def place(pair):
        return list_ref[pair] // blocks

    running_pairs(count, product, tile, peak, peak_ref, total_ref, place)
    lse_ref[...] = finished(peak_ref[0:bands], total_ref[0:bands])
    tall_copy.wait()


def col_kernel(
    bands, blocks, groups, list_ref, count_ref, src_hbm, tall_hbm, log_ref, *refs,
):
    row_refs, refs = refs[:groups], refs[groups:]
    (
        lse_ref, row_ref,
        joined_ref, src_ref, tgt_tall_ref, arrived, src_wide_ref, tile, peak, peak_ref, total_ref,
    ) = refs
    unit = unit_rows(BLOCK)
    src_copy = pltpu.make_async_copy(src_hbm, src_ref, arrived.at[0])
    tall_copy = pltpu.make_async_copy(tall_hbm, tgt_tall_ref, arrived.at[1])
    src_copy.start()
    tall_copy.start()
    peak_ref[...] = jnp.full(peak_ref.shape, FLOOR, jnp.float32)
    total_ref[...] = jnp.zeros(total_ref.shape, jnp.float32)

    joined_ref[...] = joined([ref[...] for ref in row_refs])

    def prepare(it, carry):
        for k in range(UNROLL):
            band = it * UNROLL + k
            cells = src_ref[:, block_rows(band)]
            at = pl.ds(band, 1)
            lift_row = LOG2E * log_ref[block_rows(band)].reshape(1, BLOCK) - joined_ref[at, :]
            row = (EPS * LN2) * lift_row + squares(cells.astype(jnp.float32))
            row_ref[block_rows(band)] = row.reshape(BLOCK)
            lift = part_rows(lift_row)
            src_wide_ref[band] = stacked(cells, cells, cells, unit, lift).T
        return carry

    src_copy.wait()
    lax.fori_loop(0, bands // UNROLL, prepare, 0)
    tall_copy.wait()

    def product(pair):
        code = list_ref[pair]
        band = jnp.minimum(code // blocks, bands - 1)
        return jnp.dot(src_wide_ref[band], tgt_tall_ref[code % blocks], preferred_element_type=jnp.float32)

    def place(pair):
        code = list_ref[pair]
        return jnp.where(code >= bands * blocks, blocks, code % blocks)

    running_pairs(count_ref[0], product, tile, peak, peak_ref, total_ref, place)
    sums = finished(peak_ref[0:blocks], total_ref[0:blocks])
    for block in range(blocks):
        lse_ref[block * BLOCK:(block + 1) * BLOCK] = sums[block:block + 1, :].reshape(BLOCK)


def spread(size):
    return sorted(range(1, size), key=lambda s: (-min(s, size - s), s))


def turned(value, axis, size, move):
    return lax.ppermute(value, axis, [(k, move(k)) for k in range(size)])


def shards(src_dims, sources, targets, log_src, log_tgt, tgt_potential, pattern):
    bands, slots = pattern.shape
    blocks = targets.shape[0] // BLOCK
    groups = lax.axis_size("tgt")
    own = pattern - lax.axis_index("tgt") * blocks
    code = jnp.arange(bands, dtype=jnp.int32)[:, None] * blocks + own
    ids = jnp.where((own >= 0) & (own < blocks), code, -1).T
    vmem = pl.BlockSpec(memory_space=pltpu.VMEM)
    smem = pl.BlockSpec(memory_space=pltpu.SMEM)
    hbm = pl.BlockSpec(memory_space=pl.ANY)
    params = pltpu.CompilerParams(vmem_limit_bytes=VMEM_LIMIT)

    def scratch(wide, places, *extra):
        return [
            pltpu.VMEM(sources.shape[::-1], jnp.bfloat16),
            *extra,
            pltpu.VMEM((blocks, WIDTH, BLOCK), jnp.bfloat16),
            pltpu.SemaphoreType.DMA((3,)),
            pltpu.VMEM((wide, BLOCK, WIDTH), jnp.bfloat16),
            pltpu.VMEM((GROUP, BLOCK, BLOCK), jnp.float32),
            pltpu.VMEM((GROUP, 8, BLOCK), jnp.float32),
            pltpu.VMEM((places + 1, 8, BLOCK), jnp.float32),
            pltpu.VMEM((places + 1, 8, BLOCK), jnp.float32),
        ]

    row_lse, tgt_tall, pairs, count = pl.pallas_call(
        functools.partial(row_kernel, bands, slots, blocks),
        out_shape=(
            jax.ShapeDtypeStruct((bands, BLOCK), jnp.float32),
            jax.ShapeDtypeStruct((blocks, WIDTH, BLOCK), jnp.bfloat16),
            jax.ShapeDtypeStruct((bands * slots + PAD,), jnp.int32),
            jax.ShapeDtypeStruct((1,), jnp.int32),
        ),
        in_specs=[smem, hbm, hbm, vmem],
        out_specs=(vmem, hbm, smem, smem),
        scratch_shapes=scratch(blocks, bands, pltpu.VMEM(targets.shape[::-1], jnp.bfloat16)),
        compiler_params=params,
    )(ids, sources.T, targets.T, tgt_potential)

    others = [turned(row_lse, "tgt", groups, lambda k, s=s: (k + s) % groups) for s in spread(groups)]
    col_lse, row_potential = pl.pallas_call(
        functools.partial(col_kernel, bands, blocks, groups),
        out_shape=(
            jax.ShapeDtypeStruct((blocks * BLOCK,), jnp.float32),
            jax.ShapeDtypeStruct((bands * BLOCK,), jnp.float32),
        ),
        in_specs=[smem, smem, hbm, hbm, vmem] + [vmem] * groups,
        out_specs=(vmem, vmem),
        scratch_shapes=[pltpu.VMEM((bands, BLOCK), jnp.float32)] + scratch(bands, blocks),
        compiler_params=params,
    )(pairs, count, sources.T, tgt_tall, log_src, row_lse, *others)

    size = lax.axis_size("src")
    stride = 1
    for dim in reversed(src_dims):

        def shifted(k, s, dim=dim, stride=stride):
            here = (k // stride) % dim
            return k + ((here + s) % dim - here) * stride

        col_lse = joined(
            [col_lse] + [turned(col_lse, "src", size, lambda k, s=s: shifted(k, s)) for s in spread(dim)]
        )
        stride *= dim
    col_potential = EPS * log_tgt - (EPS * LN2) * col_lse + tgt_potential
    return (row_potential, col_potential)


def src_factors(size):
    side = math.isqrt(size // 2)
    return (side, size // 2 // side, 2)


def solution(mesh):
    in_specs = (P("src", None), P("tgt", None), P("src"), P("tgt"), P("tgt"), P("src", None))
    out_specs = (P("src"), P("tgt"))
    body = functools.partial(shards, src_factors(mesh.shape["src"]))
    return jax.shard_map(body, mesh=mesh, in_specs=in_specs, out_specs=out_specs, check_vma=False)
```

```python
import functools
import math

import jax
import jax.numpy as jnp
from jax import lax
from jax.experimental import pallas as pl
from jax.experimental.pallas import tpu as pltpu
from jax.sharding import PartitionSpec as P

BLOCK = 256
EPS = 0.05
FLOOR = -1e30
LOG2E = math.log2(math.e)
LN2 = math.log(2.0)
RATE = LOG2E / EPS
GROUP = 24
UNROLL = 4
WIDTH = 256
PAD = 2 * GROUP
VMEM_LIMIT = 56 * 2**20


def three_parts(value):
    first = value.astype(jnp.bfloat16)
    rest = value - first.astype(jnp.float32)
    second = rest.astype(jnp.bfloat16)
    third = (rest - second.astype(jnp.float32)).astype(jnp.bfloat16)
    return first, second, third


def part_rows(row):
    parts = [p.astype(jnp.float32) for p in three_parts(row)]
    at = lax.broadcasted_iota(jnp.int32, (8, row.shape[-1]), 0)
    rows = jnp.zeros((8, row.shape[-1]), jnp.float32)
    for k, part in enumerate(parts):
        rows = jnp.where(at == k, part, rows)
    return rows


def unit_rows(width):
    at = lax.broadcasted_iota(jnp.int32, (8, width), 0)
    return jnp.where(at < 3, 1.0, 0.0).astype(jnp.float32)


def stacked(first, second, third, first_rows, second_rows):
    extra = jnp.concatenate([first_rows, second_rows], axis=0).astype(jnp.bfloat16)
    blank = jnp.zeros((WIDTH - 208, extra.shape[1]), jnp.bfloat16)
    return jnp.concatenate([first, second, third, extra, blank], axis=0)


def squares(wide):
    return jnp.sum(wide * wide, axis=0, keepdims=True)


def block_rows(index):
    return pl.ds(pl.multiple_of(index * BLOCK, BLOCK), BLOCK)


def running_pairs(count, product, tile, peak, peak_ref, total_ref, place):
    def first_stage(pair, slot):
        values = product(pair)
        tile[slot] = values
        peak[slot] = jnp.max(values.reshape(BLOCK // 8, 8, BLOCK), axis=0)

    def second_stage(pair, slot):
        at = place(pair)
        old = peak_ref[at]
        new = jnp.maximum(old, peak[slot])
        peak_ref[at] = new
        scale = jnp.exp2(old - new)
        total = 0.0
        for k in range(0, BLOCK, 64):
            shifted = tile[slot, k:k + 64].reshape(8, 8, BLOCK) - new[None]
            total = total + jnp.sum(jnp.exp2(shifted), axis=0)
        total_ref[at] = total_ref[at] * scale + total

    for slot in range(GROUP):
        first_stage(slot, slot)

    def step(it, carry):
        start = it * GROUP
        for slot in range(GROUP):
            second_stage(start + slot, slot)
            first_stage(start + GROUP + slot, slot)
        return carry

    lax.fori_loop(0, (count + GROUP - 1) // GROUP, step, 0)


def finished(peak, total):
    top = jnp.max(peak, axis=1)
    scaled = jnp.sum(total * jnp.exp2(peak - top[:, None, :]), axis=1)
    return top + jnp.log2(jnp.maximum(scaled, 1e-37))


def joined(values):
    top = functools.reduce(jnp.maximum, values)
    return top + jnp.log2(sum(jnp.exp2(v - top) for v in values))


def row_kernel(
    bands, slots, blocks, ids_ref, src_hbm, tgt_hbm, pot_ref,
    lse_ref, tall_hbm, list_ref, count_ref,
    src_ref, tgt_ref, tgt_tall_ref, arrived, tgt_wide_ref, tile, peak, peak_ref, total_ref,
):
    unit = unit_rows(BLOCK)
    tgt_copy = pltpu.make_async_copy(tgt_hbm, tgt_ref, arrived.at[0])
    src_copy = pltpu.make_async_copy(src_hbm, src_ref, arrived.at[1])
    tall_copy = pltpu.make_async_copy(tgt_tall_ref, tall_hbm, arrived.at[2])
    tgt_copy.start()
    src_copy.start()

    def widen_target(block):
        wide = tgt_ref[:, block_rows(block)].astype(jnp.float32)
        parts = three_parts(wide * (2.0 * RATE))
        height = RATE * (pot_ref[block_rows(block)].reshape(1, BLOCK) - squares(wide))
        tall = stacked(*parts, part_rows(height), unit)
        tgt_tall_ref[block] = tall
        tgt_wide_ref[block] = tall.T

    def list_band(band, count):
        for slot in range(slots):
            code = ids_ref[slot, band]
            list_ref[count] = code
            count = count + 1 + lax.shift_right_arithmetic(code, 31)
        return count

    each = bands // blocks * UNROLL

    def prepare(it, count):
        for k in range(UNROLL):
            widen_target(it * UNROLL + k)
        for k in range(each):
            count = list_band(it * each + k, count)
        return count

    peak_ref[...] = jnp.full(peak_ref.shape, FLOOR, jnp.float32)
    total_ref[...] = jnp.zeros(total_ref.shape, jnp.float32)
    tgt_copy.wait()
    count = lax.fori_loop(0, blocks // UNROLL, prepare, jnp.int32(0))
    for k in range(PAD):
        list_ref[count + k] = bands * blocks
    count_ref[0] = count
    tall_copy.start()
    src_copy.wait()

    def product(pair):
        code = list_ref[pair]
        band = jnp.minimum(code // blocks, bands - 1)
        cells = src_ref[:, block_rows(band)]
        tall = stacked(cells, cells, cells, unit, jnp.zeros_like(unit))
        return jnp.dot(tgt_wide_ref[code % blocks], tall, preferred_element_type=jnp.float32)

    def place(pair):
        return list_ref[pair] // blocks

    running_pairs(count, product, tile, peak, peak_ref, total_ref, place)
    lse_ref[...] = finished(peak_ref[0:bands], total_ref[0:bands])
    tall_copy.wait()


def col_kernel(
    bands, blocks, groups, list_ref, count_ref, src_hbm, tall_hbm, log_ref, *refs,
):
    row_refs, refs = refs[:groups], refs[groups:]
    (
        lse_ref, row_ref,
        joined_ref, src_ref, tgt_tall_ref, arrived, src_wide_ref, tile, peak, peak_ref, total_ref,
    ) = refs
    unit = unit_rows(BLOCK)
    src_copy = pltpu.make_async_copy(src_hbm, src_ref, arrived.at[0])
    tall_copy = pltpu.make_async_copy(tall_hbm, tgt_tall_ref, arrived.at[1])
    src_copy.start()
    tall_copy.start()
    peak_ref[...] = jnp.full(peak_ref.shape, FLOOR, jnp.float32)
    total_ref[...] = jnp.zeros(total_ref.shape, jnp.float32)

    joined_rows = joined([ref[...] for ref in row_refs])
    joined_ref[...] = joined_rows

    def prepare(it, carry):
        for k in range(UNROLL):
            band = it * UNROLL + k
            cells = src_ref[:, block_rows(band)]
            at = pl.ds(band, 1)
            lift_row = LOG2E * log_ref[block_rows(band)].reshape(1, BLOCK) - joined_ref[at, :]
            row = (EPS * LN2) * lift_row + squares(cells.astype(jnp.float32))
            row_ref[block_rows(band)] = row.reshape(BLOCK)
            lift = part_rows(lift_row)
            src_wide_ref[band] = stacked(cells, cells, cells, unit, lift).T
        return carry

    src_copy.wait()
    lax.fori_loop(0, bands // UNROLL, prepare, 0)
    tall_copy.wait()

    def product(pair):
        code = list_ref[pair]
        band = jnp.minimum(code // blocks, bands - 1)
        return jnp.dot(src_wide_ref[band], tgt_tall_ref[code % blocks], preferred_element_type=jnp.float32)

    def place(pair):
        code = list_ref[pair]
        return jnp.where(code >= bands * blocks, blocks, code % blocks)

    running_pairs(count_ref[0], product, tile, peak, peak_ref, total_ref, place)
    lse_ref[...] = finished(peak_ref[0:blocks], total_ref[0:blocks])


def spread(size):
    return sorted(range(1, size), key=lambda s: (-min(s, size - s), s))


def turned(value, axis, size, move):
    return lax.ppermute(value, axis, [(k, move(k)) for k in range(size)])


def shards(src_dims, sources, targets, log_src, log_tgt, tgt_potential, pattern):
    bands, slots = pattern.shape
    blocks = targets.shape[0] // BLOCK
    groups = lax.axis_size("tgt")
    own = pattern - lax.axis_index("tgt") * blocks
    code = jnp.arange(bands, dtype=jnp.int32)[:, None] * blocks + own
    ids = jnp.where((own >= 0) & (own < blocks), code, -1).T
    pot_blocks = tgt_potential.reshape(blocks, BLOCK)
    vmem = pl.BlockSpec(memory_space=pltpu.VMEM)
    smem = pl.BlockSpec(memory_space=pltpu.SMEM)
    hbm = pl.BlockSpec(memory_space=pl.ANY)
    params = pltpu.CompilerParams(vmem_limit_bytes=VMEM_LIMIT)

    def scratch(wide, places, *extra):
        return [
            pltpu.VMEM(sources.shape[::-1], jnp.bfloat16),
            *extra,
            pltpu.VMEM((blocks, WIDTH, BLOCK), jnp.bfloat16),
            pltpu.SemaphoreType.DMA((3,)),
            pltpu.VMEM((wide, BLOCK, WIDTH), jnp.bfloat16),
            pltpu.VMEM((GROUP, BLOCK, BLOCK), jnp.float32),
            pltpu.VMEM((GROUP, 8, BLOCK), jnp.float32),
            pltpu.VMEM((places + 1, 8, BLOCK), jnp.float32),
            pltpu.VMEM((places + 1, 8, BLOCK), jnp.float32),
        ]

    row_lse, tgt_tall, pairs, count = pl.pallas_call(
        functools.partial(row_kernel, bands, slots, blocks),
        out_shape=(
            jax.ShapeDtypeStruct((bands, BLOCK), jnp.float32),
            jax.ShapeDtypeStruct((blocks, WIDTH, BLOCK), jnp.bfloat16),
            jax.ShapeDtypeStruct((bands * slots + PAD,), jnp.int32),
            jax.ShapeDtypeStruct((1,), jnp.int32),
        ),
        in_specs=[smem, hbm, hbm, vmem],
        out_specs=(vmem, hbm, smem, smem),
        scratch_shapes=scratch(blocks, bands, pltpu.VMEM(targets.shape[::-1], jnp.bfloat16)),
        compiler_params=params,
    )(ids, sources.T, targets.T, tgt_potential)

    others = [turned(row_lse, "tgt", groups, lambda k, s=s: (k + s) % groups) for s in spread(groups)]
    col_lse, row_potential = pl.pallas_call(
        functools.partial(col_kernel, bands, blocks, groups),
        out_shape=(
            jax.ShapeDtypeStruct((blocks, BLOCK), jnp.float32),
            jax.ShapeDtypeStruct((bands * BLOCK,), jnp.float32),
        ),
        in_specs=[smem, smem, hbm, hbm, vmem] + [vmem] * groups,
        out_specs=(vmem, vmem),
        scratch_shapes=[pltpu.VMEM((bands, BLOCK), jnp.float32)] + scratch(bands, blocks),
        compiler_params=params,
    )(pairs, count, sources.T, tgt_tall, log_src, row_lse, *others)

    size = lax.axis_size("src")
    stride = 1
    for dim in reversed(src_dims):

        def shifted(k, s, dim=dim, stride=stride):
            here = (k // stride) % dim
            return k + ((here + s) % dim - here) * stride

        col_lse = joined(
            [col_lse] + [turned(col_lse, "src", size, lambda k, s=s: shifted(k, s)) for s in spread(dim)]
        )
        stride *= dim
    col_potential = EPS * log_tgt.reshape(blocks, BLOCK) - (EPS * LN2) * col_lse + pot_blocks
    return (row_potential, col_potential.reshape(-1))


def src_factors(size):
    side = math.isqrt(size // 2)
    return (side, size // 2 // side, 2)


def solution(mesh):
    in_specs = (P("src", None), P("tgt", None), P("src"), P("tgt"), P("tgt"), P("src", None))
    out_specs = (P("src"), P("tgt"))
    body = functools.partial(shards, src_factors(mesh.shape["src"]))
    return jax.shard_map(body, mesh=mesh, in_specs=in_specs, out_specs=out_specs, check_vma=False)
```
